128 devices in a mesh: row: 8 (over y_hi, x), col: 16 (over z, y_lo, core).
Axes of the slice: x: 4, y: 4 (y_hi: 2, y_lo: 2; y = y_hi * 2 + y_lo), z: 4, core: 2. Of those that a mesh axis runs over, the one named last changes fastest.
Arguments:
- weight: bfloat16 [14336, 53248], P(('row', 'col')), may hold values from -0.046875 to 0.046875
- start: float32 [53248, 64], P(('col', 'row')), may hold values from -6 to 6
Outputs:
- adapter_left: float32 [14336, 128], P(('row', 'col'))
- adapter_right: float32 [53248, 128], P(('col', 'row'))
- residual_weight: bfloat16 [14336, 53248], P(None, ('col', 'row'))
The draws below stay inside these ranges and needn't reach their ends.
All inputs are finite; a program needn't handle non-finite values.
Results may differ from the reference program's by a relative error of at most 0.01155.
Values may be sent and summed in bfloat16 or wider, within the bound.
A program may use at most 128 MiB of HBM per device.

```python
import jax
import jax.numpy as jnp
from jax import lax

N = 53248
M = 14336
BLOCK = 64
STEPS = 3
RANK = 128
SWEEPS = 4


def block_scale(stream_key, extent, cuts, smallest, largest):
    def one(position, blocks):
        draws = jax.random.uniform(jax.random.fold_in(jax.random.fold_in(stream_key, 6), position), (blocks,), jnp.float32, smallest / len(cuts), largest / len(cuts))
        return jnp.repeat(jnp.exp(draws), extent[position] // blocks).reshape((-1,) + (1,) * (len(extent) - position - 1))

    level = one(*cuts[0])
    for cut in cuts[1:]:
        level = level * one(*cut)
    return level


def normal_values(rng, shape, scale, reach, shards=(), held_as=jnp.bfloat16):
    drawn = scale * jax.random.normal(rng, shape, jnp.float32)
    if shards:
        drawn = drawn * block_scale(rng, shape, shards, -0.22, 0.18)
    return jnp.clip(drawn, -reach, reach).astype(held_as)


def setup_inputs(seed: int = 0) -> dict:
    keys = jax.random.split(jax.random.key(seed), 3)
    return {
        "weight": normal_values(keys[0], (M, N), M ** -0.5, 0.046875, ((0, 128),)),
        "start": normal_values(keys[1], (N, BLOCK), 1.0, 6.0, ((0, 128),), jnp.float32),
    }


HIGHEST = lax.Precision.HIGHEST

def product(left_side, right_side):
    return jnp.dot(left_side.astype(jnp.float32), right_side.astype(jnp.float32), precision=HIGHEST, preferred_element_type=jnp.float32)

def inner_product(left_side, right_side):
    return lax.dot_general(left_side.astype(jnp.float32), right_side.astype(jnp.float32), (((0,), (0,)), ((), ())), precision=HIGHEST, preferred_element_type=jnp.float32)

def orthonormal(matrix):
    factor = jnp.linalg.cholesky(inner_product(matrix, matrix))
    return jax.scipy.linalg.solve_triangular(factor, matrix.T, lower=True).T

def project_out(matrix, earlier):
    coefficients = inner_product(earlier, matrix)
    return orthonormal(matrix - product(earlier, coefficients))

def reference(weight, start):
    right_list = [orthonormal(start)]
    left_list = []
    image_list = []
    for turn_index in range(STEPS):
        low_right = right_list[-1].astype(jnp.bfloat16)
        image_block = jnp.dot(weight.astype(jnp.float32), low_right.astype(jnp.float32), preferred_element_type=jnp.float32)
        if turn_index == 0:
            left_list.append(orthonormal(image_block))
        else:
            left_list.append(project_out(image_block, jnp.concatenate(left_list, 1)))
        low_left = left_list[-1].astype(jnp.bfloat16)
        back_block = lax.dot_general(weight.astype(jnp.float32), low_left.astype(jnp.float32), (((0,), (0,)), ((), ())), preferred_element_type=jnp.float32)
        image_list.append(back_block)
        if turn_index + 1 < STEPS:
            right_list.append(project_out(back_block, jnp.concatenate(right_list, 1)))
    krylov = jnp.concatenate(image_list, 1)
    gram_matrix = inner_product(krylov, krylov)
    subspace_basis = jnp.eye(krylov.shape[1], dtype=jnp.float32)[:, :RANK]
    for sweep_index in range(SWEEPS):
        subspace_basis = orthonormal(product(gram_matrix, subspace_basis))
    left_factor = product(jnp.concatenate(left_list, 1), subspace_basis)
    right_factor = product(krylov, subspace_basis)
    low_left = left_factor.astype(jnp.bfloat16)
    low_right = right_factor.astype(jnp.bfloat16)
    pieces = 8
    weight_blocks = weight.reshape(pieces, M // pieces, N)
    left_blocks = low_left.reshape(pieces, M // pieces, RANK)

    def one_block(pair):
        weight_rows, left_rows = pair
        update = lax.dot_general(left_rows.astype(jnp.float32), low_right.astype(jnp.float32), (((1,), (1,)), ((), ())), preferred_element_type=jnp.float32)
        return (weight_rows.astype(jnp.float32) - update).astype(jnp.bfloat16)
    residual_weight = lax.map(one_block, (weight_blocks, left_blocks)).reshape(M, N)
    return (left_factor, right_factor, residual_weight)
```

```python
import functools

import jax
import jax.numpy as jnp
from jax import lax
from jax.experimental import pallas as pl
from jax.experimental.pallas import tpu as pltpu
from jax.sharding import PartitionSpec as P

STEPS = 3
RANK = 128
SWEEPS = 4
B = 64
LANES = 128

NX, NYH, NYL, NZ, NC = 4, 2, 2, 4, 2
ROWS, COLS = 112, 416

HIGHEST = lax.Precision.HIGHEST
MESH = pl.DeviceIdType.MESH
F32 = jnp.float32
BF16 = jnp.bfloat16
NT = (((1,), (1,)), ((), ()))
NN = (((1,), (0,)), ((), ()))

RSC, RSZ, RSY, RSX, AGX, AGY, AGZ, AGC, ARC, ARZ, ARY, ARX, ARB = range(13)


def dot(left, right, dims=NN):
    return lax.dot_general(left, right, dims, precision=HIGHEST, preferred_element_type=F32)


def fast(left, right, dims=NN):
    return lax.dot_general(left, right, dims, preferred_element_type=F32)


def inverse_factor(gram):
    sub = lax.broadcasted_iota(jnp.int32, (B, 2 * B), 0)
    lane = lax.broadcasted_iota(jnp.int32, (B, 2 * B), 1)
    wide = jnp.concatenate([gram, jnp.zeros_like(gram)], 1)
    wide = jnp.where(lane == sub + B, 1.0, wide)

    def step(k, carry):
        wide, pivots = carry
        row = jnp.sum(jnp.where(sub == k, wide, 0.0), axis=0, keepdims=True)
        pivot = row[:, 0:1]
        scaled = row * (1.0 / pivot)
        column = jnp.where(sub[:, 0:1] > k, wide[:, 0:1], 0.0)
        wide = wide - column * scaled
        pivots = jnp.where(sub == k, pivot, pivots)
        return pltpu.roll(wide, 2 * B - 1, 1), pivots

    wide, pivots = lax.fori_loop(0, B, step, (wide, jnp.ones((B, 2 * B), F32)))
    return wide[:, :B] * lax.rsqrt(pivots[:, :B])


def chain_kernel(start_ref, weight_ref, gathered, left_ref, image_ref, gram_ref, coef_ref,
                 w, core_out, core_in, z_out, z_in, y_out, y_in, x_out, x_in, acc,
                 ar_out, ar_in, right, raw, own, load_sem, send_sem, recv_sem):
    ny = NYH * NYL
    slab = ny * NX
    row_id = lax.axis_index("row")
    col_id = lax.axis_index("col")
    y_hi, x = row_id // NX, row_id % NX
    z, y_lo, core = col_id // (NYL * NC), (col_id // NC) % NYL, col_id % NC
    y = y_hi * NYL + y_lo

    def device(core, z, y, x):
        return ((y // NYL) * NX + x, (z * NYL + y % NYL) * NC + core)

    def peer(axis, d):
        if axis == "c":
            return device((core + d) % NC, z, y, x)
        if axis == "z":
            return device(core, (z + d) % NZ, y, x)
        if axis == "y":
            return device(core, z, (y + d) % ny, x)
        return device(core, z, y, (x + d) % NX)

    sizes = {"c": NC, "z": NZ, "y": ny, "x": NX}
    peers = [(a, d) for a in "czyx" for d in range(1, sizes[a])]

    def load(p, _):
        pc, pz, py, px = p // (NZ * slab), (p // slab) % NZ, (p // NX) % ny, p % NX
        dr, dc = device(pc, pz, py, px)
        pltpu.make_async_copy(weight_ref.at[dr * (NZ * NYL * NC) + dc], w.at[p, pl.ds(0, ROWS)], load_sem).start()
        return 0

    lax.fori_loop(0, NC * NZ * slab, load, 0)

    barrier = pltpu.get_barrier_semaphore()
    for a, d in peers:
        pl.semaphore_signal(barrier, inc=1, device_id=peer(a, d), device_id_type=MESH)
    pl.semaphore_wait(barrier, len(peers))

    def send_to(target, src, dst, j, phase, d):
        copy = pltpu.make_async_remote_copy(
            src_ref=src, dst_ref=dst, send_sem=send_sem.at[j, phase, d], recv_sem=recv_sem.at[j, phase, d],
            device_id=target, device_id_type=MESH)
        copy.start()
        return copy

    def send(src, dst, j, phase, d, axis):
        return send_to(peer(axis, d), src, dst, j, phase, d)

    def swap(src, dst, j, phase, d):
        return send_to(peer("c", 1), src, dst, j, phase, d)

    w[:, ROWS:, :] = jnp.zeros((NC * NZ * slab, LANES - ROWS, COLS), BF16)

    half = B // NC
    others = {"z": ARZ, "y": ARY, "x": ARX}

    class Reduce:
        def __init__(self, value, j):
            self.j, self.lanes, self.stage = j, value.shape[1], 0
            self.sent = []
            pad = -self.lanes % LANES
            if pad:
                value = jnp.concatenate([value, jnp.zeros((B, pad), F32)], 1)
            self.width = value.shape[1]
            out = ar_out.at[j, 0]
            out[:, : self.width] = value
            mine = pl.ds(pl.multiple_of(core * half, half), half)
            theirs = pl.ds(pl.multiple_of((1 - core) * half, half), half)
            self.mine = mine
            self.pending = [send(ar_out.at[j, 0, theirs, pl.ds(0, self.width)],
                                 ar_in.at[j, 0, 0, pl.ds(0, half), pl.ds(0, self.width)], j, ARC, 1, "c")]
            self.own = out[mine, : self.width]

        def step(self):
            j, width, s = self.j, self.width, self.stage
            total = self.own
            for i, copy in enumerate(self.pending):
                copy.wait_recv()
                if s < 4:
                    total = total + ar_in[j, s, i, 0:half, 0:width]
            self.sent += self.pending
            self.pending = []
            self.stage += 1
            if s < 3:
                axis = "zyx"[s]
                self.own = total
                ar_out[j, s + 1, 0:half, 0:width] = total
                for d in range(1, sizes[axis]):
                    self.pending.append(send(
                        ar_out.at[j, s + 1, pl.ds(0, half), pl.ds(0, width)],
                        ar_in.at[j, s + 1, d - 1, pl.ds(0, half), pl.ds(0, width)], j, others[axis], d, axis))
            elif s == 3:
                ar_in[j, 4, 0, self.mine, 0:width] = total
                there = ar_in.at[j, 4, 0, self.mine, pl.ds(0, width)]
                self.pending.append(send(there, there, j, ARB, 1, "c"))
            else:
                return ar_in[j, 4, 0, :, 0 : self.lanes]
            return None

    def product_slab(low, base):
        def run(put):
            step = min(8, slab)

            def body(g, _):
                block = w[pl.ds(base + g * step, step)].reshape(step * LANES, COLS)
                out = fast(low, block, NT)
                for i in range(step):
                    put(g * step + i, out[:, i * LANES : (i + 1) * LANES])
                return 0

            lax.fori_loop(0, slab // step, body, 0)
        return run

    def base_of(c, zz):
        return (c * NZ + zz) * slab

    pltpu.make_async_copy(weight_ref, w.at[:, pl.ds(0, ROWS)], load_sem).wait()

    raw[...] = start_ref[...]
    coef_ref[...] = jnp.zeros_like(coef_ref)
    z_order = [d % NZ for d in range(1, NZ + 1)]
    for j in range(STEPS):
        done = []
        low = raw[...].astype(BF16)
        right[j * B : (j + 1) * B, :] = raw[...]
        gram = dot(raw[...], right[0 : (j + 1) * B, :], NT)
        if j:
            newest = image_ref[(j - 1) * B : j * B, :]
            gram = jnp.concatenate([gram, dot(newest, image_ref[0 : j * B, :], NT)], 1)
        reduce = Reduce(gram, j)

        core_copies = {}
        for d in z_order:
            def put(i, value, d=d):
                core_out[d, i] = value.astype(BF16)
            product_slab(low, base_of(1 - core, (z + d) % NZ))(put)
            core_copies[d] = swap(core_out.at[d], core_in.at[j, d], j, RSC, d)
        reduce.step()
        z_copies = []
        for d in z_order:
            def put(i, value):
                acc[i] = value
            product_slab(low, base_of(core, (z + d) % NZ))(put)
            core_copies[d].wait_recv()
            if d:
                z_out[d - 1] = (acc[...] + core_in[j, d].astype(F32)).astype(BF16)
                z_copies.append(send(z_out.at[d - 1], z_in.at[j, d - 1], j, RSZ, d, "z"))
            else:
                acc[...] = acc[...] + core_in[j, d].astype(F32)
        done += list(core_copies.values()) + z_copies
        reduce.step()
        reduce.step()
        reduce.step()
        total = reduce.step()
        done += reduce.sent

        cross = total[:, 0 : j * B]
        clean = total[:, j * B : (j + 1) * B]
        if j:
            gram_ref[(j - 1) * B : j * B, 0 : j * B] = total[:, (j + 1) * B : (2 * j + 1) * B]
            clean = clean - dot(cross, cross, NT)
        solve = inverse_factor(clean)
        block = raw[...]
        if j:
            block = block - dot(cross, right[0 : j * B, :])
        right[j * B : (j + 1) * B, :] = dot(solve, block)

        for copy in z_copies:
            copy.wait_recv()
        y_copies = []
        for d in range(1, ny + 1):
            e = d % ny
            at = pl.ds(((y + e) % ny) * NX, NX)
            value = acc[at]
            for i in range(NZ - 1):
                value = value + z_in[j, i, at].astype(F32)
            if e:
                y_out[e - 1] = value
                y_copies.append(send(y_out.at[e - 1], y_in.at[j, e - 1], j, RSY, e, "y"))
            else:
                acc[at] = value
        for copy in y_copies:
            copy.wait_recv()
        x_copies = []
        for d in range(1, NX + 1):
            e = d % NX
            at = (x + e) % NX
            value = acc[y * NX + at]
            for i in range(ny - 1):
                value = value + y_in[j, i, at]
            if e:
                x_out[e - 1] = value
                x_copies.append(send(x_out.at[e - 1], x_in.at[j, e - 1], j, RSX, e, "x"))
            else:
                mine = value
        for i, copy in enumerate(x_copies):
            copy.wait_recv()
            mine = mine + x_in[j, i]
        done += y_copies + x_copies
        if j:
            mine = mine - dot(cross, own[0 : j * B, :])
        mine = dot(solve, mine)
        own[j * B : (j + 1) * B, :] = mine

        place = ((core * NZ + z) * ny + y) * NX + x
        gathered[j, place] = mine.astype(BF16)

        def spread(axis, phase, at, n):
            piece = gathered.at[j, pl.ds(at, n)]
            return [send(piece, piece, j, phase, d, axis) for d in range(1, sizes[axis])]

        for axis, phase, at, n in (("x", AGX, place, 1), ("y", AGY, place - x, NX)):
            copies = spread(axis, phase, at, n)
            for copy in copies:
                copy.wait_recv()
            done += copies
        copies = spread("z", AGZ, base_of(core, z), slab)
        done += copies

        def back_slab(carry, base):
            step = min(8, slab)

            def body(g, carry):
                image, gram = carry
                at = pl.ds(base + g * step, step)
                pieces = [gathered[j, base + g * step + i] for i in range(step)]
                newest = jnp.concatenate(pieces, 1)
                image = image + fast(newest, w[at].reshape(step * LANES, COLS))
                grams = []
                for k in range(j + 1):
                    piece = newest if k == j else jnp.concatenate(
                        [gathered[k, base + g * step + i] for i in range(step)], 1)
                    grams.append(gram[k] + fast(newest, piece, NT))
                return image, tuple(grams)

            return lax.fori_loop(0, slab // step, body, carry)

        def handed(d):
            piece = gathered.at[j, pl.ds(base_of(core, (z + d) % NZ), slab)]
            return swap(piece, piece, j, AGC, d)

        carry = (jnp.zeros((B, COLS), F32), tuple(jnp.zeros((B, B), F32) for _ in range(j + 1)))
        handed_on = {0: handed(0)}
        carry = back_slab(carry, base_of(core, z))
        for d in range(1, NZ):
            copies[d - 1].wait_recv()
            handed_on[(NZ - d) % NZ] = handed((NZ - d) % NZ)
            carry = back_slab(carry, base_of(core, (z + NZ - d) % NZ))
        for d in [0] + [(NZ - d) % NZ for d in range(1, NZ)]:
            handed_on[d].wait_recv()
            carry = back_slab(carry, base_of(1 - core, (z + d) % NZ))
        done += list(handed_on.values())
        image, grams = carry

        clean = grams[j]
        if j:
            table = coef_ref[0 : j * B, 0 : j * B]
            cross = dot(jnp.concatenate(grams[:j], 1), table, NT)
            clean = clean - dot(cross, cross, NT)
        solve = inverse_factor(clean)
        if j:
            image = image - dot(cross, image_ref[0 : j * B, :])
        image = dot(solve, image)
        image_ref[j * B : (j + 1) * B, :] = image
        if j + 1 < STEPS:
            raw[...] = image - dot(dot(solve, clean), right[j * B : (j + 1) * B, :])
        left = mine
        if j:
            left = left - dot(cross, left_ref[0 : j * B, :])
            coef_ref[j * B : (j + 1) * B, 0 : j * B] = -dot(solve, dot(cross, table))
        left_ref[j * B : (j + 1) * B, :] = dot(solve, left)
        coef_ref[j * B : (j + 1) * B, j * B : (j + 1) * B] = solve
        for copy in done:
            copy.wait_send()

    reduce = Reduce(dot(image_ref[(STEPS - 1) * B :, :], image_ref[...], NT), STEPS)
    total = None
    while total is None:
        total = reduce.step()
    gram_ref[(STEPS - 1) * B :, :] = total
    for copy in reduce.sent:
        copy.wait_send()


def chain(start_t, blocks):
    ny = NYH * NYL
    slab = ny * NX
    n = NC * NZ * slab
    vmem = pl.BlockSpec(memory_space=pltpu.VMEM)
    s = STEPS * B
    return pl.pallas_call(
        chain_kernel,
        out_shape=(
            jax.ShapeDtypeStruct((STEPS, n, B, LANES), BF16),
            jax.ShapeDtypeStruct((s, LANES), F32),
            jax.ShapeDtypeStruct((s, COLS), F32),
            jax.ShapeDtypeStruct((s, s), F32),
            jax.ShapeDtypeStruct((s, s), F32),
        ),
        in_specs=[vmem, pl.BlockSpec(memory_space=pl.ANY)],
        out_specs=[vmem] * 5,
        scratch_shapes=[
            pltpu.VMEM((n, LANES, COLS), BF16),
            pltpu.VMEM((NZ, slab, B, LANES), BF16),
            pltpu.VMEM((STEPS, NZ, slab, B, LANES), BF16),
            pltpu.VMEM((NZ - 1, slab, B, LANES), BF16),
            pltpu.VMEM((STEPS, NZ - 1, slab, B, LANES), BF16),
            pltpu.VMEM((ny - 1, NX, B, LANES), F32),
            pltpu.VMEM((STEPS, ny - 1, NX, B, LANES), F32),
            pltpu.VMEM((NX - 1, B, LANES), F32),
            pltpu.VMEM((STEPS, NX - 1, B, LANES), F32),
            pltpu.VMEM((slab, B, LANES), F32),
            pltpu.VMEM((STEPS + 1, 4, B, 3 * LANES), F32),
            pltpu.VMEM((STEPS + 1, 5, 3, B, 3 * LANES), F32),
            pltpu.VMEM((s, COLS), F32),
            pltpu.VMEM((B, COLS), F32),
            pltpu.VMEM((s, LANES), F32),
            pltpu.SemaphoreType.DMA,
            pltpu.SemaphoreType.DMA((STEPS + 1, 13, 4)),
            pltpu.SemaphoreType.DMA((STEPS + 1, 13, 4)),
        ],
        compiler_params=pltpu.CompilerParams(
            collective_id=0, has_side_effects=True, vmem_limit_bytes=60 * 1024 * 1024),
    )(start_t, blocks)


def sweep_kernel(gram_ref, coef_ref, basis_ref, high_ref, low_ref):
    g = [[None] * STEPS for _ in range(STEPS)]
    for i in range(STEPS):
        for k in range(i + 1):
            g[i][k] = gram_ref[i * B : (i + 1) * B, k * B : (k + 1) * B]
            if k < i:
                g[k][i] = g[i][k].T
    whole = jnp.concatenate([jnp.concatenate(r, 1) for r in g], 0)

    def orth(grown):
        top, bottom = grown[:B], grown[B:]
        one = inverse_factor(dot(top, top, NT))
        first = dot(one, top)
        cross = dot(bottom, first, NT)
        clean = bottom - dot(cross, first)
        two = inverse_factor(dot(clean, clean, NT))
        return jnp.concatenate([first, dot(two, clean)], 0)

    basis = orth(whole[:RANK])
    basis = lax.fori_loop(1, SWEEPS, lambda _, basis: orth(dot(basis, whole)), basis)
    basis_ref[...] = basis
    mixed = dot(basis, coef_ref[...])
    high = mixed.astype(BF16)
    high_ref[...] = high
    low_ref[...] = (mixed - high.astype(F32)).astype(BF16)


def sweeps(gram, coef):
    s = STEPS * B
    return pl.pallas_call(
        sweep_kernel,
        out_shape=(
            jax.ShapeDtypeStruct((RANK, s), F32),
            jax.ShapeDtypeStruct((RANK, s), BF16),
            jax.ShapeDtypeStruct((RANK, s), BF16),
        ),
    )(gram, coef)


PER = 8


def residual_kernel(gathered, high, low, right, weight, out):
    ny = NYH * NYL
    first = pl.program_id(0) * PER
    pieces = []
    for i in range(PER):
        at = first + i
        r, c = at // (NZ * NYL * NC), at % (NZ * NYL * NC)
        place = (((c % NC) * NZ + c // (NYL * NC)) * ny + (r // NX) * NYL + (c // NC) % NYL) * NX + r % NX
        pieces.append(jnp.concatenate([gathered[k, place] for k in range(STEPS)], 0))
    stacked = jnp.concatenate(pieces, 1)
    left = (fast(high[...], stacked) + fast(low[...], stacked)).astype(BF16).T
    update = fast(left, right[...], NT)
    for i in range(PER):
        out[i * ROWS : (i + 1) * ROWS, :] = (
            weight[i].astype(F32) - update[i * LANES : i * LANES + ROWS, :]).astype(BF16)


def residual(gathered, high, low, right, blocks):
    n = blocks.shape[0]
    whole = lambda a: pl.BlockSpec(a.shape, lambda i: (0,) * a.ndim)
    return pl.pallas_call(
        residual_kernel,
        grid=(n // PER,),
        out_shape=jax.ShapeDtypeStruct((n * ROWS, COLS), BF16),
        in_specs=[whole(gathered), whole(high), whole(low), whole(right),
                  pl.BlockSpec((PER, ROWS, COLS), lambda i: (i, 0, 0))],
        out_specs=pl.BlockSpec((PER * ROWS, COLS), lambda i: (i, 0)),
        compiler_params=pltpu.CompilerParams(vmem_limit_bytes=48 * 1024 * 1024),
    )(gathered, high, low, right, blocks)


def shards(weight, start):
    rows, cols = NYH * NX, NZ * NYL * NC
    n = rows * cols
    parts = weight.reshape(ROWS, cols, rows, COLS).transpose(2, 1, 0, 3).reshape(n, ROWS, COLS)
    blocks = lax.all_to_all(parts, ("row", "col"), split_axis=0, concat_axis=0, tiled=True)
    gathered, left, images, gram, coef = chain(start.T, blocks)
    basis, high, low = sweeps(gram, coef)
    adapter_left = lax.dot_general(left[:, :ROWS], basis, (((0,), (1,)), ((), ())), precision=HIGHEST,
                                   preferred_element_type=F32)
    adapter_right = lax.dot_general(images, basis, (((0,), (1,)), ((), ())), precision=HIGHEST,
                                    preferred_element_type=F32)
    out = residual(gathered, high, low, adapter_right.astype(BF16), blocks)
    return (adapter_left, adapter_right, out)


def solution(mesh):
    return jax.shard_map(
        shards,
        mesh=mesh,
        in_specs=(P(("row", "col"), None), P(("col", "row"), None)),
        out_specs=(P(("row", "col"), None), P(("col", "row"), None), P(None, ("col", "row"))),
        check_vma=False,
    )
```

```python
import functools

import jax
import jax.numpy as jnp
from jax import lax
from jax.experimental import pallas as pl
from jax.experimental.pallas import tpu as pltpu
from jax.sharding import PartitionSpec as P

STEPS = 3
RANK = 128
SWEEPS = 4
B = 64
LANES = 128

NX, NYH, NYL, NZ, NC = 4, 2, 2, 4, 2
ROWS, COLS = 112, 416

HIGHEST = lax.Precision.HIGHEST
MESH = pl.DeviceIdType.MESH
F32 = jnp.float32
BF16 = jnp.bfloat16
NT = (((1,), (1,)), ((), ()))
NN = (((1,), (0,)), ((), ()))

RSC, RSZ, RSY, RSX, AGX, AGY, AGZ, AGC, ARC, ARZ, ARY, ARX, ARB = range(13)


def dot(left, right, dims=NN):
    return lax.dot_general(left, right, dims, precision=HIGHEST, preferred_element_type=F32)


def fast(left, right, dims=NN):
    return lax.dot_general(left, right, dims, preferred_element_type=F32)


def inverse_factor(gram):
    sub = lax.broadcasted_iota(jnp.int32, (8, LANES), 0)
    lane = lax.broadcasted_iota(jnp.int32, (8, LANES), 1)
    wide = jnp.concatenate([gram, jnp.zeros_like(gram)], 1)
    n = B // 8
    rows = [jnp.where(lane == sub + (B + 8 * q), 1.0, wide[8 * q : 8 * q + 8]) for q in range(n)]
    for p in range(n):
        columns = {q: [jnp.broadcast_to(rows[q][:, 8 * p + k : 8 * p + k + 1], (8, LANES)) for k in range(8)]
                   for q in range(p, n)}
        scale = jnp.ones((8, LANES), F32)
        for k in range(8):
            pivot = columns[p][k][k : k + 1]
            inverse = 1.0 / pivot
            scale = jnp.where(sub == k, lax.rsqrt(pivot), scale)
            row = rows[p][k : k + 1] * inverse
            ahead = {i: columns[p][i][k : k + 1] * inverse for i in range(k + 1, 8)}
            for q in range(p, n):
                factor = columns[q][k]
                if q == p:
                    factor = jnp.where(sub > k, factor, 0.0)
                rows[q] = rows[q] - factor * row
                for i in range(k + 1, 8):
                    columns[q][i] = columns[q][i] - factor * ahead[i]
        rows[p] = rows[p] * scale
    return jnp.concatenate(rows, 0)[:, B:]


def chain_kernel(start_ref, weight_ref, gathered, left_ref, image_ref, gram_ref, coef_ref,
                 w, core_out, core_in, z_out, z_in, y_out, y_in, x_out, x_in, acc,
                 ar_out, ar_in, right, raw, own, load_sem, send_sem, recv_sem):
    ny = NYH * NYL
    slab = ny * NX
    row_id = lax.axis_index("row")
    col_id = lax.axis_index("col")
    y_hi, x = row_id // NX, row_id % NX
    z, y_lo, core = col_id // (NYL * NC), (col_id // NC) % NYL, col_id % NC
    y = y_hi * NYL + y_lo

    def device(core, z, y, x):
        return ((y // NYL) * NX + x, (z * NYL + y % NYL) * NC + core)

    def peer(axis, d):
        if axis == "c":
            return device((core + d) % NC, z, y, x)
        if axis == "z":
            return device(core, (z + d) % NZ, y, x)
        if axis == "y":
            return device(core, z, (y + d) % ny, x)
        return device(core, z, y, (x + d) % NX)

    sizes = {"c": NC, "z": NZ, "y": ny, "x": NX}
    peers = [(a, d) for a in "czyx" for d in range(1, sizes[a])]

    def load(p, _):
        pc, pz, py, px = p // (NZ * slab), (p // slab) % NZ, (p // NX) % ny, p % NX
        dr, dc = device(pc, pz, py, px)
        pltpu.make_async_copy(weight_ref.at[dr * (NZ * NYL * NC) + dc], w.at[p], load_sem).start()
        return 0

    lax.fori_loop(0, NC * NZ * slab, load, 0)

    barrier = pltpu.get_barrier_semaphore()
    for a, d in peers:
        pl.semaphore_signal(barrier, inc=1, device_id=peer(a, d), device_id_type=MESH)
    pl.semaphore_wait(barrier, len(peers))

    def send_to(target, src, dst, j, phase, d):
        copy = pltpu.make_async_remote_copy(
            src_ref=src, dst_ref=dst, send_sem=send_sem.at[j, phase, d], recv_sem=recv_sem.at[j, phase, d],
            device_id=target, device_id_type=MESH)
        copy.start()
        return copy

    def send(src, dst, j, phase, d, axis):
        return send_to(peer(axis, d), src, dst, j, phase, d)

    def swap(src, dst, j, phase, d):
        return send_to(peer("c", 1), src, dst, j, phase, d)

    half = B // NC
    others = {"z": ARZ, "y": ARY, "x": ARX}

    class Reduce:
        def __init__(self, value, j):
            self.j, self.lanes, self.stage = j, value.shape[1], 0
            self.sent = []
            pad = -self.lanes % LANES
            if pad:
                value = jnp.concatenate([value, jnp.zeros((B, pad), F32)], 1)
            self.width = value.shape[1]
            out = ar_out.at[j, 0]
            out[:, : self.width] = value
            mine = pl.ds(pl.multiple_of(core * half, half), half)
            theirs = pl.ds(pl.multiple_of((1 - core) * half, half), half)
            self.mine = mine
            self.pending = [send(ar_out.at[j, 0, theirs, pl.ds(0, self.width)],
                                 ar_in.at[j, 0, 0, pl.ds(0, half), pl.ds(0, self.width)], j, ARC, 1, "c")]
            self.own = out[mine, : self.width]

        def step(self):
            j, width, s = self.j, self.width, self.stage
            total = self.own
            for i, copy in enumerate(self.pending):
                copy.wait_recv()
                if s < 4:
                    total = total + ar_in[j, s, i, 0:half, 0:width]
            self.sent += self.pending
            self.pending = []
            self.stage += 1
            if s < 3:
                axis = "zyx"[s]
                self.own = total
                ar_out[j, s + 1, 0:half, 0:width] = total
                for d in range(1, sizes[axis]):
                    self.pending.append(send(
                        ar_out.at[j, s + 1, pl.ds(0, half), pl.ds(0, width)],
                        ar_in.at[j, s + 1, d - 1, pl.ds(0, half), pl.ds(0, width)], j, others[axis], d, axis))
            elif s == 3:
                ar_in[j, 4, 0, self.mine, 0:width] = total
                there = ar_in.at[j, 4, 0, self.mine, pl.ds(0, width)]
                self.pending.append(send(there, there, j, ARB, 1, "c"))
            else:
                return ar_in[j, 4, 0, :, 0 : self.lanes]
            return None

    def product_slab(low, base):
        def run(put):
            step = min(8, slab)

            def body(g, _):
                block = jnp.concatenate([w[base + g * step + i] for i in range(step)], 1)
                out = fast(low, block)
                for i in range(step):
                    put(g * step + i, out[:, i * LANES : (i + 1) * LANES])
                return 0

            lax.fori_loop(0, slab // step, body, 0)
        return run

    def base_of(c, zz):
        return (c * NZ + zz) * slab

    pltpu.make_async_copy(weight_ref, w, load_sem).wait()

    raw[...] = start_ref[...]
    coef_ref[...] = jnp.zeros_like(coef_ref)
    z_order = [d % NZ for d in range(1, NZ + 1)]
    for j in range(STEPS):
        done = []
        low = raw[...].astype(BF16)
        right[j * B : (j + 1) * B, :] = raw[...]
        gram = dot(raw[...], right[0 : (j + 1) * B, :], NT)
        if j:
            newest = image_ref[(j - 1) * B : j * B, :]
            gram = jnp.concatenate([gram, dot(newest, image_ref[0 : j * B, :], NT)], 1)
        reduce = Reduce(gram, j)

        core_copies = {}
        for d in z_order:
            def put(i, value, d=d):
                core_out[d, i] = value.astype(BF16)
            product_slab(low, base_of(1 - core, (z + d) % NZ))(put)
            core_copies[d] = swap(core_out.at[d], core_in.at[j, d], j, RSC, d)
        reduce.step()
        z_copies = []
        for d in z_order:
            def put(i, value):
                acc[i] = value
            product_slab(low, base_of(core, (z + d) % NZ))(put)
            core_copies[d].wait_recv()
            if d:
                z_out[d - 1] = (acc[...] + core_in[j, d].astype(F32)).astype(BF16)
                z_copies.append(send(z_out.at[d - 1], z_in.at[j, d - 1], j, RSZ, d, "z"))
            else:
                acc[...] = acc[...] + core_in[j, d].astype(F32)
        done += list(core_copies.values()) + z_copies
        reduce.step()
        reduce.step()
        reduce.step()
        total = reduce.step()
        done += reduce.sent

        cross = total[:, 0 : j * B]
        clean = total[:, j * B : (j + 1) * B]
        if j:
            gram_ref[(j - 1) * B : j * B, 0 : j * B] = total[:, (j + 1) * B : (2 * j + 1) * B]
            clean = clean - dot(cross, cross, NT)
        solve = inverse_factor(clean)
        block = raw[...]
        if j:
            block = block - dot(cross, right[0 : j * B, :])
        right[j * B : (j + 1) * B, :] = dot(solve, block)

        for copy in z_copies:
            copy.wait_recv()
        y_copies = []
        for d in range(1, ny + 1):
            e = d % ny
            at = pl.ds(((y + e) % ny) * NX, NX)
            value = acc[at]
            for i in range(NZ - 1):
                value = value + z_in[j, i, at].astype(F32)
            if e:
                y_out[e - 1] = value
                y_copies.append(send(y_out.at[e - 1], y_in.at[j, e - 1], j, RSY, e, "y"))
            else:
                acc[at] = value
        for copy in y_copies:
            copy.wait_recv()
        x_copies = []
        for d in range(1, NX + 1):
            e = d % NX
            at = (x + e) % NX
            value = acc[y * NX + at]
            for i in range(ny - 1):
                value = value + y_in[j, i, at]
            if e:
                x_out[e - 1] = value
                x_copies.append(send(x_out.at[e - 1], x_in.at[j, e - 1], j, RSX, e, "x"))
            else:
                mine = value
        for i, copy in enumerate(x_copies):
            copy.wait_recv()
            mine = mine + x_in[j, i]
        done += y_copies + x_copies
        if j:
            mine = mine - dot(cross, own[0 : j * B, :])
        mine = dot(solve, mine)
        own[j * B : (j + 1) * B, :] = mine

        place = ((core * NZ + z) * ny + y) * NX + x
        gathered[j, place] = mine.astype(BF16)

        def spread(axis, phase, at, n):
            piece = gathered.at[j, pl.ds(at, n)]
            return [send(piece, piece, j, phase, d, axis) for d in range(1, sizes[axis])]

        for axis, phase, at, n in (("x", AGX, place, 1), ("y", AGY, place - x, NX)):
            copies = spread(axis, phase, at, n)
            for copy in copies:
                copy.wait_recv()
            done += copies
        copies = spread("z", AGZ, base_of(core, z), slab)
        done += copies

        def back_slab(carry, base):
            step = min(8, slab)

            def body(g, carry):
                image, gram = carry
                pieces = [gathered[j, base + g * step + i] for i in range(step)]
                newest = jnp.concatenate(pieces, 1)
                block = jnp.concatenate([w[base + g * step + i] for i in range(step)], 1)
                image = image + fast(newest, block, NT)
                grams = []
                for k in range(j + 1):
                    piece = newest if k == j else jnp.concatenate(
                        [gathered[k, base + g * step + i] for i in range(step)], 1)
                    grams.append(gram[k] + fast(newest, piece, NT))
                return image, tuple(grams)

            return lax.fori_loop(0, slab // step, body, carry)

        def handed(d):
            piece = gathered.at[j, pl.ds(base_of(core, (z + d) % NZ), slab)]
            return swap(piece, piece, j, AGC, d)

        carry = (jnp.zeros((B, COLS), F32), tuple(jnp.zeros((B, B), F32) for _ in range(j + 1)))
        handed_on = {0: handed(0)}
        carry = back_slab(carry, base_of(core, z))
        for d in range(1, NZ):
            copies[d - 1].wait_recv()
            handed_on[(NZ - d) % NZ] = handed((NZ - d) % NZ)
            carry = back_slab(carry, base_of(core, (z + NZ - d) % NZ))
        for d in [0] + [(NZ - d) % NZ for d in range(1, NZ)]:
            handed_on[d].wait_recv()
            carry = back_slab(carry, base_of(1 - core, (z + d) % NZ))
        done += list(handed_on.values())
        image, grams = carry

        clean = grams[j]
        if j:
            table = coef_ref[0 : j * B, 0 : j * B]
            cross = dot(jnp.concatenate(grams[:j], 1), table, NT)
            clean = clean - dot(cross, cross, NT)
        solve = inverse_factor(clean)
        if j:
            image = image - dot(cross, image_ref[0 : j * B, :])
        image = dot(solve, image)
        image_ref[j * B : (j + 1) * B, :] = image
        if j + 1 < STEPS:
            raw[...] = image - dot(dot(solve, clean), right[j * B : (j + 1) * B, :])
        left = mine
        if j:
            left = left - dot(cross, left_ref[0 : j * B, :])
            coef_ref[j * B : (j + 1) * B, 0 : j * B] = -dot(solve, dot(cross, table))
        left_ref[j * B : (j + 1) * B, :] = dot(solve, left)
        coef_ref[j * B : (j + 1) * B, j * B : (j + 1) * B] = solve
        for copy in done:
            copy.wait_send()

    reduce = Reduce(dot(image_ref[(STEPS - 1) * B :, :], image_ref[...], NT), STEPS)
    total = None
    while total is None:
        total = reduce.step()
    gram_ref[(STEPS - 1) * B :, :] = total
    for copy in reduce.sent:
        copy.wait_send()


def chain(start_t, blocks):
    ny = NYH * NYL
    slab = ny * NX
    n = NC * NZ * slab
    vmem = pl.BlockSpec(memory_space=pltpu.VMEM)
    s = STEPS * B
    return pl.pallas_call(
        chain_kernel,
        out_shape=(
            jax.ShapeDtypeStruct((STEPS, n, B, LANES), BF16),
            jax.ShapeDtypeStruct((s, LANES), F32),
            jax.ShapeDtypeStruct((s, COLS), F32),
            jax.ShapeDtypeStruct((s, s), F32),
            jax.ShapeDtypeStruct((s, s), F32),
        ),
        in_specs=[vmem, pl.BlockSpec(memory_space=pl.ANY)],
        out_specs=[vmem] * 5,
        scratch_shapes=[
            pltpu.VMEM((n, COLS, LANES), BF16),
            pltpu.VMEM((NZ, slab, B, LANES), BF16),
            pltpu.VMEM((STEPS, NZ, slab, B, LANES), BF16),
            pltpu.VMEM((NZ - 1, slab, B, LANES), BF16),
            pltpu.VMEM((STEPS, NZ - 1, slab, B, LANES), BF16),
            pltpu.VMEM((ny - 1, NX, B, LANES), F32),
            pltpu.VMEM((STEPS, ny - 1, NX, B, LANES), F32),
            pltpu.VMEM((NX - 1, B, LANES), F32),
            pltpu.VMEM((STEPS, NX - 1, B, LANES), F32),
            pltpu.VMEM((slab, B, LANES), F32),
            pltpu.VMEM((STEPS + 1, 4, B, 3 * LANES), F32),
            pltpu.VMEM((STEPS + 1, 5, 3, B, 3 * LANES), F32),
            pltpu.VMEM((s, COLS), F32),
            pltpu.VMEM((B, COLS), F32),
            pltpu.VMEM((s, LANES), F32),
            pltpu.SemaphoreType.DMA,
            pltpu.SemaphoreType.DMA((STEPS + 1, 13, 4)),
            pltpu.SemaphoreType.DMA((STEPS + 1, 13, 4)),
        ],
        compiler_params=pltpu.CompilerParams(
            collective_id=0, has_side_effects=True, vmem_limit_bytes=60 * 1024 * 1024),
    )(start_t, blocks)


def sweep_kernel(gram_ref, coef_ref, basis_ref, high_ref, low_ref):
    g = [[None] * STEPS for _ in range(STEPS)]
    for i in range(STEPS):
        for k in range(i + 1):
            g[i][k] = gram_ref[i * B : (i + 1) * B, k * B : (k + 1) * B]
            if k < i:
                g[k][i] = g[i][k].T
    whole = jnp.concatenate([jnp.concatenate(r, 1) for r in g], 0)

    def orth(grown):
        top, bottom = grown[:B], grown[B:]
        one = inverse_factor(dot(top, top, NT))
        first = dot(one, top)
        cross = dot(bottom, first, NT)
        clean = bottom - dot(cross, first)
        two = inverse_factor(dot(clean, clean, NT))
        return jnp.concatenate([first, dot(two, clean)], 0)

    basis = orth(whole[:RANK])
    basis = lax.fori_loop(1, SWEEPS, lambda _, basis: orth(dot(basis, whole)), basis)
    basis_ref[...] = basis
    mixed = dot(basis, coef_ref[...])
    high = mixed.astype(BF16)
    high_ref[...] = high
    low_ref[...] = (mixed - high.astype(F32)).astype(BF16)


def sweeps(gram, coef):
    s = STEPS * B
    return pl.pallas_call(
        sweep_kernel,
        out_shape=(
            jax.ShapeDtypeStruct((RANK, s), F32),
            jax.ShapeDtypeStruct((RANK, s), BF16),
            jax.ShapeDtypeStruct((RANK, s), BF16),
        ),
    )(gram, coef)


PER = 8


def residual_kernel(gathered, high, low, right, weight, out):
    ny = NYH * NYL
    first = pl.program_id(0) * PER
    pieces = []
    for i in range(PER):
        at = first + i
        r, c = at // (NZ * NYL * NC), at % (NZ * NYL * NC)
        place = (((c % NC) * NZ + c // (NYL * NC)) * ny + (r // NX) * NYL + (c // NC) % NYL) * NX + r % NX
        pieces.append(jnp.concatenate([gathered[k, place] for k in range(STEPS)], 0))
    stacked = jnp.concatenate(pieces, 1)
    left = (fast(high[...], stacked) + fast(low[...], stacked)).astype(BF16).T
    left = jnp.concatenate([left[i * LANES : i * LANES + ROWS] for i in range(PER)], 0)
    update = fast(right[...], left, NT)
    lane = lax.broadcasted_iota(jnp.int32, (COLS, LANES), 1)
    gap = LANES - ROWS
    for t in range(PER * ROWS // LANES):
        block = weight[t].astype(F32)
        if t:
            block = pltpu.roll(block, LANES - gap * t, 1)
        after = pltpu.roll(weight[t + 1].astype(F32), ROWS - gap * t, 1)
        block = jnp.where(lane < ROWS - gap * t, block, after)
        at = slice(t * LANES, (t + 1) * LANES)
        out[:, at] = (block - update[:, at]).astype(BF16)


def residual(gathered, high, low, right, blocks):
    n = blocks.shape[0]
    whole = lambda a: pl.BlockSpec(a.shape, lambda i: (0,) * a.ndim)
    return pl.pallas_call(
        residual_kernel,
        grid=(n // PER,),
        out_shape=jax.ShapeDtypeStruct((COLS, n * ROWS), BF16),
        in_specs=[whole(gathered), whole(high), whole(low), whole(right),
                  pl.BlockSpec((PER, COLS, LANES), lambda i: (i, 0, 0))],
        out_specs=pl.BlockSpec((COLS, PER * ROWS), lambda i: (0, i)),
        compiler_params=pltpu.CompilerParams(vmem_limit_bytes=48 * 1024 * 1024),
    )(gathered, high, low, right, blocks)


def shards(weight, start):
    rows, cols = NYH * NX, NZ * NYL * NC
    n = rows * cols
    padded = jnp.pad(weight, ((0, LANES - ROWS), (0, 0)))
    parts = padded.T.reshape(cols, rows, COLS, LANES).transpose(1, 0, 2, 3).reshape(n, COLS, LANES)
    blocks = lax.all_to_all(parts, ("row", "col"), split_axis=0, concat_axis=0, tiled=True)
    gathered, left, images, gram, coef = chain(start.T, blocks)
    basis, high, low = sweeps(gram, coef)
    adapter_left = lax.dot_general(left[:, :ROWS], basis, (((0,), (1,)), ((), ())), precision=HIGHEST,
                                   preferred_element_type=F32)
    adapter_right = lax.dot_general(images, basis, (((0,), (1,)), ((), ())), precision=HIGHEST,
                                    preferred_element_type=F32)
    out = residual(gathered, high, low, adapter_right.astype(BF16), blocks)
    return (adapter_left, adapter_right, out.T)


def solution(mesh):
    return jax.shard_map(
        shards,
        mesh=mesh,
        in_specs=(P(("row", "col"), None), P(("col", "row"), None)),
        out_specs=(P(("row", "col"), None), P(("col", "row"), None), P(None, ("col", "row"))),
        check_vma=False,
    )
```

```python
import functools

import jax
import jax.numpy as jnp
from jax import lax
from jax.experimental import pallas as pl
from jax.experimental.pallas import tpu as pltpu
from jax.sharding import PartitionSpec as P

STEPS = 3
RANK = 128
SWEEPS = 4
B = 64
LANES = 128

NX, NYH, NYL, NZ, NC = 4, 2, 2, 4, 2
ROWS, COLS = 112, 416

HIGHEST = lax.Precision.HIGHEST
MESH = pl.DeviceIdType.MESH
F32 = jnp.float32
BF16 = jnp.bfloat16
NT = (((1,), (1,)), ((), ()))
NN = (((1,), (0,)), ((), ()))

STREAMS = ((0, 32, "zyx"), (32, 48, "yxz"), (48, 64, "xzy"))
RSC, RS, AG, AGC, ARC, ARZ, ARY, ARX, ARB = 0, 1, 10, 19, 20, 21, 22, 23, 24
EXCHANGES = 25


def dot(left, right, dims=NN):
    return lax.dot_general(left, right, dims, precision=HIGHEST, preferred_element_type=F32)


def fast(left, right, dims=NN):
    return lax.dot_general(left, right, dims, preferred_element_type=F32)


def inverse_factor(gram):
    sub = lax.broadcasted_iota(jnp.int32, (8, LANES), 0)
    lane = lax.broadcasted_iota(jnp.int32, (8, LANES), 1)
    wide = jnp.concatenate([gram, jnp.zeros_like(gram)], 1)
    n = B // 8
    rows = [jnp.where(lane == sub + (B + 8 * q), 1.0, wide[8 * q : 8 * q + 8]) for q in range(n)]
    for p in range(n):
        columns = {q: [jnp.broadcast_to(rows[q][:, 8 * p + k : 8 * p + k + 1], (8, LANES)) for k in range(8)]
                   for q in range(p, n)}
        scale = jnp.ones((8, LANES), F32)
        for k in range(8):
            pivot = columns[p][k][k : k + 1]
            inverse = 1.0 / pivot
            scale = jnp.where(sub == k, lax.rsqrt(pivot), scale)
            row = rows[p][k : k + 1] * inverse
            ahead = {i: columns[p][i][k : k + 1] * inverse for i in range(k + 1, 8)}
            for q in range(p, n):
                factor = columns[q][k]
                if q == p:
                    factor = jnp.where(sub > k, factor, 0.0)
                rows[q] = rows[q] - factor * row
                for i in range(k + 1, 8):
                    columns[q][i] = columns[q][i] - factor * ahead[i]
        rows[p] = rows[p] * scale
    return jnp.concatenate(rows, 0)[:, B:]


def chain_kernel(start_ref, weight_ref, gathered, left_ref, image_ref, gram_ref, coef_ref, blocks_ref,
                 w, strip, staged, core_out, core_in, out1, in1, out2, in2, out3, in3, acc,
                 ar_out, ar_in, right, raw, own, strip_sem, keep_sem, put_sem, get_sem, send_sem, recv_sem):
    ny = NYH * NYL
    slab = ny * NX
    n = NC * NZ * slab
    row_id = lax.axis_index("row")
    col_id = lax.axis_index("col")
    y_hi, x = row_id // NX, row_id % NX
    z, y_lo, core = col_id // (NYL * NC), (col_id // NC) % NYL, col_id % NC
    y = y_hi * NYL + y_lo
    here = {"z": z, "y": y, "x": x}
    sizes = {"c": NC, "z": NZ, "y": ny, "x": NX}

    def device(core, z, y, x):
        return ((y // NYL) * NX + x, (z * NYL + y % NYL) * NC + core)

    def spot(core, z, y, x):
        return ((core * NZ + z) * ny + y) * NX + x

    def peer(axis, d):
        if axis == "c":
            return device((core + d) % NC, z, y, x)
        if axis == "z":
            return device(core, (z + d) % NZ, y, x)
        if axis == "y":
            return device(core, z, (y + d) % ny, x)
        return device(core, z, y, (x + d) % NX)

    place = spot(core, z, y, x)

    groups = n // NX

    def offset(i):
        step, g = i // ny, i % ny
        return step // NZ, (g + step % NZ) % NZ, g

    def strip_copy(i):
        dc, dz, dy = offset(i)
        dr, dl = device((core + dc) % NC, (z + dz) % NZ, (y + dy) % ny, 0)
        block = dl * (NYH * NX) + dr
        return pltpu.make_async_copy(
            weight_ref.at[:, pl.ds(pl.multiple_of(block * COLS, LANES), NX * COLS)], strip.at[i % 2],
            strip_sem.at[i % 2])

    def block_copy(i, dx):
        dc, dz, dy = offset(i)
        tx = (x + dx) % NX
        return pltpu.make_async_remote_copy(
            src_ref=staged.at[i, tx], dst_ref=w.at[place], send_sem=put_sem.at[i, dx], recv_sem=get_sem.at[i, dx],
            device_id=device((core + dc) % NC, (z + dz) % NZ, (y + dy) % ny, tx), device_id_type=MESH)

    strip_copy(0).start()
    barrier = pltpu.get_barrier_semaphore()

    def greet(d, _):
        to = (place + d) % n
        target = device(to // (NZ * slab), (to // slab) % NZ, (to // NX) % ny, to % NX)
        pl.semaphore_signal(barrier, inc=1, device_id=target, device_id_type=MESH)
        return 0

    lax.fori_loop(1, n, greet, 0)

    def stage(i):
        strip_copy(i).wait()

        @pl.when(i < groups - 1)
        def _():
            strip_copy(i + 1).start()

        value = strip[i % 2]
        value = jnp.concatenate([value, jnp.zeros((LANES - ROWS, NX * COLS), BF16)], 0).T
        staged[i] = value.reshape(NX, COLS, LANES)

    def scatter(step, _):
        def each(g, _):
            stage(step * ny + g)
            return 0

        lax.fori_loop(0, ny, each, 0)

        @pl.when(step == 0)
        def _():
            pl.semaphore_wait(barrier, n - 1)
            pltpu.make_async_copy(staged.at[0, x], w.at[place], keep_sem).start()

        def rotate(a, _):
            for dx in range(NX):
                i = step * ny + (dx + a) % ny
                if dx == 0:
                    @pl.when(i != 0)
                    def _():
                        block_copy(i, dx).start()
                else:
                    block_copy(i, dx).start()
            return 0

        lax.fori_loop(0, ny, rotate, 0)
        return 0

    lax.fori_loop(0, groups // ny, scatter, 0)

    def send_to(target, src, dst, j, phase, d):
        copy = pltpu.make_async_remote_copy(
            src_ref=src, dst_ref=dst, send_sem=send_sem.at[j, phase, d], recv_sem=recv_sem.at[j, phase, d],
            device_id=target, device_id_type=MESH)
        copy.start()
        return copy

    def send(src, dst, j, phase, d, axis):
        return send_to(peer(axis, d), src, dst, j, phase, d)

    def swap(src, dst, j, phase, d):
        return send_to(peer("c", 1), src, dst, j, phase, d)

    half = B // NC
    others = {"z": ARZ, "y": ARY, "x": ARX}

    class Reduce:
        def __init__(self, value, j):
            self.j, self.lanes, self.stage = j, value.shape[1], 0
            self.sent = []
            pad = -self.lanes % LANES
            if pad:
                value = jnp.concatenate([value, jnp.zeros((B, pad), F32)], 1)
            self.width = value.shape[1]
            out = ar_out.at[j, 0]
            out[:, : self.width] = value
            mine = pl.ds(pl.multiple_of(core * half, half), half)
            theirs = pl.ds(pl.multiple_of((1 - core) * half, half), half)
            self.mine = mine
            self.pending = [send(ar_out.at[j, 0, theirs, pl.ds(0, self.width)],
                                 ar_in.at[j, 0, 0, pl.ds(0, half), pl.ds(0, self.width)], j, ARC, 1, "c")]
            self.own = out[mine, : self.width]

        def step(self):
            j, width, s = self.j, self.width, self.stage
            total = self.own
            for i, copy in enumerate(self.pending):
                copy.wait_recv()
                if s < 4:
                    total = total + ar_in[j, s, i, 0:half, 0:width]
            self.sent += self.pending
            self.pending = []
            self.stage += 1
            if s < 3:
                axis = "zyx"[s]
                self.own = total
                ar_out[j, s + 1, 0:half, 0:width] = total
                for d in range(1, sizes[axis]):
                    self.pending.append(send(
                        ar_out.at[j, s + 1, pl.ds(0, half), pl.ds(0, width)],
                        ar_in.at[j, s + 1, d - 1, pl.ds(0, half), pl.ds(0, width)], j, others[axis], d, axis))
            elif s == 3:
                ar_in[j, 4, 0, self.mine, 0:width] = total
                there = ar_in.at[j, 4, 0, self.mine, pl.ds(0, width)]
                self.pending.append(send(there, there, j, ARB, 1, "c"))
            else:
                return ar_in[j, 4, 0, :, 0 : self.lanes]
            return None

    chunk = min(8, slab)

    def product_slab(low, base, put):
        def body(g, _):
            block = jnp.concatenate([w[base + g * chunk + i] for i in range(chunk)], 1)
            out = fast(low, block)
            for i in range(chunk):
                put(g * chunk + i, out[:, i * LANES : (i + 1) * LANES])
            return 0

        lax.fori_loop(0, slab // chunk, body, 0)

    def base_of(c, zz):
        return (c * NZ + zz) * slab

    def arrive(i, _):
        for dx in range(NX):
            if dx == 0:
                @pl.when(i != 0)
                def _():
                    block_copy(i, dx).wait()
            else:
                block_copy(i, dx).wait()
        return 0

    lax.fori_loop(0, groups, arrive, 0)
    pltpu.make_async_copy(staged.at[0, x], w.at[place], keep_sem).wait()

    def keep(p, _):
        dr, dl = device(p // (NZ * slab), (p // slab) % NZ, (p // NX) % ny, p % NX)
        pltpu.make_async_copy(w.at[p], blocks_ref.at[dr * (NZ * NYL * NC) + dl], keep_sem).start()
        return 0

    lax.fori_loop(0, n, keep, 0)

    raw[...] = start_ref[...]
    coef_ref[...] = jnp.zeros_like(coef_ref)
    z_order = [d % NZ for d in range(1, NZ + 1)]
    for j in range(STEPS):
        done = []
        low = raw[...].astype(BF16)
        right[j * B : (j + 1) * B, :] = raw[...]
        gram = dot(raw[...], right[0 : (j + 1) * B, :], NT)
        if j:
            newest = image_ref[(j - 1) * B : j * B, :]
            gram = jnp.concatenate([gram, dot(newest, image_ref[0 : j * B, :], NT)], 1)
        reduce = Reduce(gram, j)

        core_copies = {}
        for d in z_order:
            def put(i, value, d=d):
                core_out[d, i] = value.astype(BF16)
            product_slab(low, base_of(1 - core, (z + d) % NZ), put)
            core_copies[d] = swap(core_out.at[d], core_in.at[j, d], j, RSC, d)
        reduce.step()
        flights = [[] for _ in STREAMS]

        def first(t, d):
            axis = STREAMS[t][2][0]
            flights[t].append(send(out1[t].at[(here[axis] + d) % sizes[axis]], in1[t].at[j, d - 1],
                                   j, RS + t, d, axis))

        for d in z_order:
            core_copies[d].wait_recv()
            at = {"z": (z + d) % NZ}

            def put(i, value, d=d, at=at):
                value = value + core_in[j, d, i].astype(F32)
                at = {"z": at["z"], "y": i // NX, "x": i % NX}
                acc[at["z"] * slab + i] = value
                for t, (lo, hi, (p, q, r)) in enumerate(STREAMS):
                    out1[t][at[p], at[q] * sizes[r] + at[r]] = value[lo:hi].astype(BF16)

            product_slab(low, base_of(core, at["z"]), put)
            if d:
                first(0, d)
        for t in (1, 2):
            for d in range(1, sizes[STREAMS[t][2][0]]):
                first(t, d)
        done += list(core_copies.values())
        reduce.step()
        second = [[] for _ in STREAMS]
        for t in (1, 2, 0):
            lo, hi, (p, q, r) = STREAMS[t]
            for copy in flights[t]:
                copy.wait_recv()

            def add(iq, _):
                for ir in range(sizes[r]):
                    at = {p: here[p], q: iq, r: ir}
                    value = acc[(at["z"] * ny + at["y"]) * NX + at["x"], lo:hi]
                    for i in range(sizes[p] - 1):
                        value = value + in1[t][j, i, iq * sizes[r] + ir].astype(F32)
                    out2[t][iq, ir] = value
                return 0

            lax.fori_loop(0, sizes[q], add, 0)
            for d in range(1, sizes[q]):
                second[t].append(send(out2[t].at[(here[q] + d) % sizes[q]], in2[t].at[j, d - 1],
                                      j, RS + 3 + t, d, q))
            done += flights[t]
        reduce.step()
        third = [[] for _ in STREAMS]
        for t in (1, 2, 0):
            lo, hi, (p, q, r) = STREAMS[t]
            for copy in second[t]:
                copy.wait_recv()
            for ir in range(sizes[r]):
                value = out2[t][here[q], ir]
                for i in range(sizes[q] - 1):
                    value = value + in2[t][j, i, ir]
                out3[t][ir] = value
            for d in range(1, sizes[r]):
                third[t].append(send(out3[t].at[(here[r] + d) % sizes[r]], in3[t].at[j, d - 1],
                                     j, RS + 6 + t, d, r))
            done += second[t]
        reduce.step()
        total = reduce.step()
        done += reduce.sent

        cross = total[:, 0 : j * B]
        clean = total[:, j * B : (j + 1) * B]
        if j:
            gram_ref[(j - 1) * B : j * B, 0 : j * B] = total[:, (j + 1) * B : (2 * j + 1) * B]
            clean = clean - dot(cross, cross, NT)
        solve = inverse_factor(clean)

        parts = []
        for t in range(len(STREAMS)):
            lo, hi, (p, q, r) = STREAMS[t]
            value = out3[t][here[r]]
            for i, copy in enumerate(third[t]):
                copy.wait_recv()
                value = value + in3[t][j, i]
            parts.append(value)
            done += third[t]
        mine = jnp.concatenate(parts, 0)
        if j:
            mine = mine - dot(cross, own[0 : j * B, :])
        mine = dot(solve, mine)
        own[j * B : (j + 1) * B, :] = mine

        gathered[j, core, z, y, x] = mine.astype(BF16)

        def spread(t, phase):
            lo, hi, (p, q, r) = STREAMS[t]
            axis = (r, q, p)[phase]
            free = ("", r, r + q)[phase]
            at = [pl.ds(0, sizes[a]) if a in free else here[a] for a in "zyx"]
            piece = gathered.at[j, core, at[0], at[1], at[2], pl.ds(lo, hi - lo)]
            return [send(piece, piece, j, AG + 3 * phase + t, d, axis) for d in range(1, sizes[axis])]

        flights = [spread(t, 0) for t in range(len(STREAMS))]
        block = raw[...]
        if j:
            block = block - dot(cross, right[0 : j * B, :])
        right[j * B : (j + 1) * B, :] = dot(solve, block)
        for phase in (1, 2):
            for t in (0, 1, 2):
                for copy in flights[t]:
                    copy.wait_recv()
                done += flights[t]
                flights[t] = spread(t, phase)
        for t in (1, 2, 0):
            for copy in flights[t]:
                copy.wait_recv()
            done += flights[t]
        handed = []
        for d in range(NZ):
            piece = gathered.at[j, core, (z + d) % NZ]
            handed.append(swap(piece, piece, j, AGC, d))
        done += handed

        def back_slab(carry, c, zz):
            def body(g, carry):
                image, gram = carry
                index = [(g * (chunk // NX) + i // NX, i % NX) for i in range(chunk)]
                newest = jnp.concatenate([gathered[j, c, zz, iy, ix] for iy, ix in index], 1)
                block = jnp.concatenate([w[base_of(c, zz) + g * chunk + i] for i in range(chunk)], 1)
                image = image + fast(newest, block, NT)
                grams = []
                for k in range(j + 1):
                    piece = newest if k == j else jnp.concatenate(
                        [gathered[k, c, zz, iy, ix] for iy, ix in index], 1)
                    grams.append(gram[k] + fast(newest, piece, NT))
                return image, tuple(grams)

            return lax.fori_loop(0, slab // chunk, body, carry)

        carry = (jnp.zeros((B, COLS), F32), tuple(jnp.zeros((B, B), F32) for _ in range(j + 1)))
        carry = lax.fori_loop(0, NZ, lambda zz, carry: back_slab(carry, core, zz), carry)
        for d in range(NZ):
            handed[d].wait_recv()
            carry = back_slab(carry, 1 - core, (z + d) % NZ)
        image, grams = carry

        clean = grams[j]
        if j:
            table = coef_ref[0 : j * B, 0 : j * B]
            cross = dot(jnp.concatenate(grams[:j], 1), table, NT)
            clean = clean - dot(cross, cross, NT)
        solve = inverse_factor(clean)
        if j:
            image = image - dot(cross, image_ref[0 : j * B, :])
        image = dot(solve, image)
        image_ref[j * B : (j + 1) * B, :] = image
        if j + 1 < STEPS:
            raw[...] = image - dot(dot(solve, clean), right[j * B : (j + 1) * B, :])
        left = mine
        if j:
            left = left - dot(cross, left_ref[0 : j * B, :])
            coef_ref[j * B : (j + 1) * B, 0 : j * B] = -dot(solve, dot(cross, table))
        left_ref[j * B : (j + 1) * B, :] = dot(solve, left)
        coef_ref[j * B : (j + 1) * B, j * B : (j + 1) * B] = solve
        for copy in done:
            copy.wait_send()

    reduce = Reduce(dot(image_ref[(STEPS - 1) * B :, :], image_ref[...], NT), STEPS)
    total = None
    while total is None:
        total = reduce.step()
    gram_ref[(STEPS - 1) * B :, :] = total
    for copy in reduce.sent:
        copy.wait_send()
    pltpu.make_async_copy(w, blocks_ref, keep_sem).wait()


def chain(start_t, weight):
    ny = NYH * NYL
    slab = ny * NX
    n = NC * NZ * slab
    vmem = pl.BlockSpec(memory_space=pltpu.VMEM)
    hbm = pl.BlockSpec(memory_space=pl.ANY)
    s = STEPS * B
    sizes = {"z": NZ, "y": ny, "x": NX}

    def buffers(shape, kind):
        return [pltpu.VMEM(shape(*(sizes[a] for a in axes)) + (hi - lo, LANES), kind) for lo, hi, axes in STREAMS]

    return pl.pallas_call(
        chain_kernel,
        out_shape=(
            jax.ShapeDtypeStruct((STEPS, NC, NZ, ny, NX, B, LANES), BF16),
            jax.ShapeDtypeStruct((s, LANES), F32),
            jax.ShapeDtypeStruct((s, COLS), F32),
            jax.ShapeDtypeStruct((s, s), F32),
            jax.ShapeDtypeStruct((s, s), F32),
            jax.ShapeDtypeStruct((n, COLS, LANES), BF16),
        ),
        in_specs=[vmem, hbm],
        out_specs=[vmem] * 5 + [hbm],
        scratch_shapes=[
            pltpu.VMEM((n, COLS, LANES), BF16),
            pltpu.VMEM((2, ROWS, NX * COLS), BF16),
            pltpu.VMEM((n // NX, NX, COLS, LANES), BF16),
            pltpu.VMEM((NZ, slab, B, LANES), BF16),
            pltpu.VMEM((STEPS, NZ, slab, B, LANES), BF16),
            buffers(lambda p, q, r: (p, q * r), BF16),
            buffers(lambda p, q, r: (STEPS, max(p - 1, 1), q * r), BF16),
            buffers(lambda p, q, r: (q, r), F32),
            buffers(lambda p, q, r: (STEPS, max(q - 1, 1), r), F32),
            buffers(lambda p, q, r: (r,), F32),
            buffers(lambda p, q, r: (STEPS, max(r - 1, 1)), F32),
            pltpu.VMEM((NZ * slab, B, LANES), F32),
            pltpu.VMEM((STEPS + 1, 4, B, 3 * LANES), F32),
            pltpu.VMEM((STEPS + 1, 5, 3, B, 3 * LANES), F32),
            pltpu.VMEM((s, COLS), F32),
            pltpu.VMEM((B, COLS), F32),
            pltpu.VMEM((s, LANES), F32),
            pltpu.SemaphoreType.DMA((2,)),
            pltpu.SemaphoreType.DMA,
            pltpu.SemaphoreType.DMA((n // NX, NX)),
            pltpu.SemaphoreType.DMA((n // NX, NX)),
            pltpu.SemaphoreType.DMA((STEPS + 1, EXCHANGES, 4)),
            pltpu.SemaphoreType.DMA((STEPS + 1, EXCHANGES, 4)),
        ],
        compiler_params=pltpu.CompilerParams(
            collective_id=0, has_side_effects=True, vmem_limit_bytes=62 * 1024 * 1024),
    )(start_t, weight)


def sweep_kernel(gram_ref, coef_ref, basis_ref, high_ref, low_ref):
    g = [[None] * STEPS for _ in range(STEPS)]
    for i in range(STEPS):
        for k in range(i + 1):
            g[i][k] = gram_ref[i * B : (i + 1) * B, k * B : (k + 1) * B]
            if k < i:
                g[k][i] = g[i][k].T
    whole = jnp.concatenate([jnp.concatenate(r, 1) for r in g], 0)

    def orth(grown):
        top, bottom = grown[:B], grown[B:]
        one = inverse_factor(dot(top, top, NT))
        first = dot(one, top)
        cross = dot(bottom, first, NT)
        clean = bottom - dot(cross, first)
        two = inverse_factor(dot(clean, clean, NT))
        return jnp.concatenate([first, dot(two, clean)], 0)

    basis = orth(whole[:RANK])
    basis = lax.fori_loop(1, SWEEPS, lambda _, basis: orth(dot(basis, whole)), basis)
    basis_ref[...] = basis
    mixed = dot(basis, coef_ref[...])
    high = mixed.astype(BF16)
    high_ref[...] = high
    low_ref[...] = (mixed - high.astype(F32)).astype(BF16)


def sweeps(gram, coef):
    s = STEPS * B
    return pl.pallas_call(
        sweep_kernel,
        out_shape=(
            jax.ShapeDtypeStruct((RANK, s), F32),
            jax.ShapeDtypeStruct((RANK, s), BF16),
            jax.ShapeDtypeStruct((RANK, s), BF16),
        ),
    )(gram, coef)


PER = 8


def residual_kernel(gathered, high, low, right, weight, out):
    first = pl.program_id(0) * PER
    pieces = []
    for i in range(PER):
        at = first + i
        r, c = at // (NZ * NYL * NC), at % (NZ * NYL * NC)
        place = (c % NC, c // (NYL * NC), (r // NX) * NYL + (c // NC) % NYL, r % NX)
        pieces.append(jnp.concatenate([gathered[(k,) + place] for k in range(STEPS)], 0))
    stacked = jnp.concatenate(pieces, 1)
    left = (fast(high[...], stacked) + fast(low[...], stacked)).astype(BF16).T
    left = jnp.concatenate([left[i * LANES : i * LANES + ROWS] for i in range(PER)], 0)
    update = fast(right[...], left, NT)
    lane = lax.broadcasted_iota(jnp.int32, (COLS, LANES), 1)
    gap = LANES - ROWS
    for t in range(PER * ROWS // LANES):
        block = weight[t].astype(F32)
        if t:
            block = pltpu.roll(block, LANES - gap * t, 1)
        after = pltpu.roll(weight[t + 1].astype(F32), ROWS - gap * t, 1)
        block = jnp.where(lane < ROWS - gap * t, block, after)
        at = slice(t * LANES, (t + 1) * LANES)
        out[:, at] = (block - update[:, at]).astype(BF16)


def residual(gathered, high, low, right, blocks):
    n = blocks.shape[0]
    whole = lambda a: pl.BlockSpec(a.shape, lambda i: (0,) * a.ndim)
    return pl.pallas_call(
        residual_kernel,
        grid=(n // PER,),
        out_shape=jax.ShapeDtypeStruct((COLS, n * ROWS), BF16),
        in_specs=[whole(gathered), whole(high), whole(low), whole(right),
                  pl.BlockSpec((PER, COLS, LANES), lambda i: (i, 0, 0))],
        out_specs=pl.BlockSpec((COLS, PER * ROWS), lambda i: (0, i)),
        compiler_params=pltpu.CompilerParams(vmem_limit_bytes=48 * 1024 * 1024),
    )(gathered, high, low, right, blocks)


def shards(weight, start):
    gathered, left, images, gram, coef, blocks = chain(start.T, weight)
    basis, high, low = sweeps(gram, coef)
    adapter_left = lax.dot_general(left[:, :ROWS], basis, (((0,), (1,)), ((), ())), precision=HIGHEST,
                                   preferred_element_type=F32)
    adapter_right = lax.dot_general(images, basis, (((0,), (1,)), ((), ())), precision=HIGHEST,
                                    preferred_element_type=F32)
    out = residual(gathered, high, low, adapter_right.astype(BF16), blocks)
    return (adapter_left, adapter_right, out.T)


def solution(mesh):
    return jax.shard_map(
        shards,
        mesh=mesh,
        in_specs=(P(("row", "col"), None), P(("col", "row"), None)),
        out_specs=(P(("row", "col"), None), P(("col", "row"), None), P(None, ("col", "row"))),
        check_vma=False,
    )
```

```python
import functools

import jax
import jax.numpy as jnp
from jax import lax
from jax.experimental import pallas as pl
from jax.experimental.pallas import tpu as pltpu
from jax.sharding import PartitionSpec as P

STEPS = 3
RANK = 128
SWEEPS = 4
B = 64
LANES = 128

NX, NYH, NYL, NZ, NC = 4, 2, 2, 4, 2
ROWS, COLS = 112, 416
GAP, TAIL = LANES - ROWS, 48
SENT = COLS - TAIL

HIGHEST = lax.Precision.HIGHEST
MESH = pl.DeviceIdType.MESH
F32 = jnp.float32
BF16 = jnp.bfloat16
NT = (((1,), (1,)), ((), ()))
NN = (((1,), (0,)), ((), ()))

STREAMS = ((0, 32, "zyx"), (32, 48, "yxz"), (48, 64, "xzy"))
RSC, RS, AG, AGC, ARC, ARZ, ARY, ARX, ARB = 0, 1, 10, 19, 20, 21, 22, 23, 24
EXCHANGES = 25


def dot(left, right, dims=NN):
    return lax.dot_general(left, right, dims, precision=HIGHEST, preferred_element_type=F32)


def fast(left, right, dims=NN):
    return lax.dot_general(left, right, dims, preferred_element_type=F32)


def inverse_factor(gram):
    sub = lax.broadcasted_iota(jnp.int32, (8, LANES), 0)
    lane = lax.broadcasted_iota(jnp.int32, (8, LANES), 1)
    wide = jnp.concatenate([gram, jnp.zeros_like(gram)], 1)
    n = B // 8
    rows = [jnp.where(lane == sub + (B + 8 * q), 1.0, wide[8 * q : 8 * q + 8]) for q in range(n)]
    for p in range(n):
        columns = {q: [jnp.broadcast_to(rows[q][:, 8 * p + k : 8 * p + k + 1], (8, LANES)) for k in range(8)]
                   for q in range(p, n)}
        scale = jnp.ones((8, LANES), F32)
        for k in range(8):
            pivot = columns[p][k][k : k + 1]
            inverse = 1.0 / pivot
            scale = jnp.where(sub == k, lax.rsqrt(pivot), scale)
            row = rows[p][k : k + 1] * inverse
            ahead = {i: columns[p][i][k : k + 1] * inverse for i in range(k + 1, 8)}
            for q in range(p, n):
                factor = columns[q][k]
                if q == p:
                    factor = jnp.where(sub > k, factor, 0.0)
                rows[q] = rows[q] - factor * row
                for i in range(k + 1, 8):
                    columns[q][i] = columns[q][i] - factor * ahead[i]
        rows[p] = rows[p] * scale
    return jnp.concatenate(rows, 0)[:, B:]


def pack(block):
    tail = block[SENT:].astype(F32)
    lane = lax.broadcasted_iota(jnp.int32, (TAIL, LANES), 1)
    pieces = []
    for m in range(ROWS // GAP):
        moved = pltpu.roll(tail, ROWS - GAP * m, 1)
        pieces.append(jnp.where(lane < ROWS, block[TAIL * m : TAIL * (m + 1)].astype(F32), moved).astype(BF16))
    return jnp.concatenate(pieces + [block[TAIL * (ROWS // GAP) : SENT]], 0)


def unpack(w, p):
    lane = lax.broadcasted_iota(jnp.int32, (TAIL, LANES), 1)
    tail = jnp.zeros((TAIL, LANES), F32)
    for m in range(ROWS // GAP):
        at = slice(TAIL * m, TAIL * (m + 1))
        piece = w[p, at].astype(F32)
        moved = pltpu.roll(piece, (LANES - ROWS + GAP * m) % LANES, 1)
        tail = jnp.where((lane >= GAP * m) & (lane < GAP * (m + 1)), moved, tail)
        w[p, at] = jnp.where(lane < ROWS, piece, 0.0).astype(BF16)
    w[p, SENT:] = tail.astype(BF16)


def chain_kernel(start_ref, weight_ref, gathered, left_ref, image_ref, gram_ref, coef_ref, blocks_ref,
                 w, strip, staged, core_out, core_in, out1, in1, out2, in2, out3, in3, acc,
                 ar_out, ar_in, right, raw, own, strip_sem, keep_sem, put_sem, get_sem, send_sem, recv_sem):
    ny = NYH * NYL
    slab = ny * NX
    n = NC * NZ * slab
    row_id = lax.axis_index("row")
    col_id = lax.axis_index("col")
    y_hi, x = row_id // NX, row_id % NX
    z, y_lo, core = col_id // (NYL * NC), (col_id // NC) % NYL, col_id % NC
    y = y_hi * NYL + y_lo
    here = {"z": z, "y": y, "x": x}
    sizes = {"c": NC, "z": NZ, "y": ny, "x": NX}

    def device(core, z, y, x):
        return ((y // NYL) * NX + x, (z * NYL + y % NYL) * NC + core)

    def spot(core, z, y, x):
        return ((core * NZ + z) * ny + y) * NX + x

    def peer(axis, d):
        if axis == "c":
            return device((core + d) % NC, z, y, x)
        if axis == "z":
            return device(core, (z + d) % NZ, y, x)
        if axis == "y":
            return device(core, z, (y + d) % ny, x)
        return device(core, z, y, (x + d) % NX)

    place = spot(core, z, y, x)

    groups = n // NX

    def offset(i):
        step, g = i // ny, i % ny
        return step // NZ, (g + step % NZ) % NZ, g

    def strip_copy(i):
        dc, dz, dy = offset(i)
        dr, dl = device((core + dc) % NC, (z + dz) % NZ, (y + dy) % ny, 0)
        block = dl * (NYH * NX) + dr
        return pltpu.make_async_copy(
            weight_ref.at[:, pl.ds(pl.multiple_of(block * COLS, LANES), NX * COLS)], strip.at[i % 2],
            strip_sem.at[i % 2])

    def block_copy(i, dx):
        dc, dz, dy = offset(i)
        tx = (x + dx) % NX
        return pltpu.make_async_remote_copy(
            src_ref=staged.at[i, tx], dst_ref=w.at[place, pl.ds(0, SENT)], send_sem=put_sem.at[i, dx], recv_sem=get_sem.at[i, dx],
            device_id=device((core + dc) % NC, (z + dz) % NZ, (y + dy) % ny, tx), device_id_type=MESH)

    strip_copy(0).start()
    barrier = pltpu.get_barrier_semaphore()

    def greet(d, _):
        to = (place + d) % n
        target = device(to // (NZ * slab), (to // slab) % NZ, (to // NX) % ny, to % NX)
        pl.semaphore_signal(barrier, inc=1, device_id=target, device_id_type=MESH)
        return 0

    lax.fori_loop(1, n, greet, 0)

    def stage(i):
        strip_copy(i).wait()

        @pl.when(i < groups - 1)
        def _():
            strip_copy(i + 1).start()

        value = strip[i % 2]
        value = jnp.concatenate([value, jnp.zeros((LANES - ROWS, NX * COLS), BF16)], 0).T
        for k in range(NX):
            staged[i, k] = pack(value[k * COLS : (k + 1) * COLS])

    def scatter(step, _):
        def each(g, _):
            stage(step * ny + g)
            return 0

        lax.fori_loop(0, ny, each, 0)

        @pl.when(step == 0)
        def _():
            pl.semaphore_wait(barrier, n - 1)
            pltpu.make_async_copy(staged.at[0, x], w.at[place, pl.ds(0, SENT)], keep_sem).start()

        def rotate(a, _):
            for dx in range(NX):
                i = step * ny + (dx + a) % ny
                if dx == 0:
                    @pl.when(i != 0)
                    def _():
                        block_copy(i, dx).start()
                else:
                    block_copy(i, dx).start()
            return 0

        lax.fori_loop(0, ny, rotate, 0)
        return 0

    lax.fori_loop(0, groups // ny, scatter, 0)

    def send_to(target, src, dst, j, phase, d):
        copy = pltpu.make_async_remote_copy(
            src_ref=src, dst_ref=dst, send_sem=send_sem.at[j, phase, d], recv_sem=recv_sem.at[j, phase, d],
            device_id=target, device_id_type=MESH)
        copy.start()
        return copy

    def send(src, dst, j, phase, d, axis):
        return send_to(peer(axis, d), src, dst, j, phase, d)

    def swap(src, dst, j, phase, d):
        return send_to(peer("c", 1), src, dst, j, phase, d)

    half = B // NC
    others = {"z": ARZ, "y": ARY, "x": ARX}

    class Reduce:
        def __init__(self, value, j):
            self.j, self.lanes, self.stage = j, value.shape[1], 0
            self.sent = []
            pad = -self.lanes % LANES
            if pad:
                value = jnp.concatenate([value, jnp.zeros((B, pad), F32)], 1)
            self.width = value.shape[1]
            out = ar_out.at[j, 0]
            out[:, : self.width] = value
            mine = pl.ds(pl.multiple_of(core * half, half), half)
            theirs = pl.ds(pl.multiple_of((1 - core) * half, half), half)
            self.mine = mine
            self.pending = [send(ar_out.at[j, 0, theirs, pl.ds(0, self.width)],
                                 ar_in.at[j, 0, 0, pl.ds(0, half), pl.ds(0, self.width)], j, ARC, 1, "c")]
            self.own = out[mine, : self.width]

        def step(self):
            j, width, s = self.j, self.width, self.stage
            total = self.own
            for i, copy in enumerate(self.pending):
                copy.wait_recv()
                if s < 4:
                    total = total + ar_in[j, s, i, 0:half, 0:width]
            self.sent += self.pending
            self.pending = []
            self.stage += 1
            if s < 3:
                axis = "zyx"[s]
                self.own = total
                ar_out[j, s + 1, 0:half, 0:width] = total
                for d in range(1, sizes[axis]):
                    self.pending.append(send(
                        ar_out.at[j, s + 1, pl.ds(0, half), pl.ds(0, width)],
                        ar_in.at[j, s + 1, d - 1, pl.ds(0, half), pl.ds(0, width)], j, others[axis], d, axis))
            elif s == 3:
                ar_in[j, 4, 0, self.mine, 0:width] = total
                there = ar_in.at[j, 4, 0, self.mine, pl.ds(0, width)]
                self.pending.append(send(there, there, j, ARB, 1, "c"))
            else:
                return ar_in[j, 4, 0, :, 0 : self.lanes]
            return None

    def product_slab(low, base, put):
        out = fast(low, jnp.concatenate([w[base + i] for i in range(slab)], 1))
        for i in range(slab):
            put(i, out[:, i * LANES : (i + 1) * LANES])

    def base_of(c, zz):
        return (c * NZ + zz) * slab

    raw[...] = start_ref[...]
    coef_ref[...] = jnp.zeros_like(coef_ref)
    start_low = raw[...].astype(BF16)
    right[0:B, :] = raw[...]
    reduce = Reduce(dot(raw[...], raw[...], NT), 0)
    pltpu.make_async_copy(staged.at[0, x], w.at[place, pl.ds(0, SENT)], keep_sem).wait()

    def arrive(i, _):
        dc, dz, dy = offset(i)
        fz, fy = (z - dz + NZ) % NZ, (y - dy + ny) % ny
        base = spot((core - dc + NC) % NC, fz, fy, 0)
        for dx in range(NX):
            if dx == 0:
                @pl.when(i != 0)
                def _():
                    block_copy(i, dx).wait()
            else:
                block_copy(i, dx).wait()
        for k in range(NX):
            unpack(w, base + k)
        out = fast(start_low, jnp.concatenate([w[base + k] for k in range(NX)], 1))

        @pl.when(dc == 0)
        def _():
            for k in range(NX):
                acc[(fz * ny + fy) * NX + k] = out[:, k * LANES : (k + 1) * LANES]

        @pl.when(dc != 0)
        def _():
            for k in range(NX):
                core_out[(NZ - dz) % NZ, fy * NX + k] = out[:, k * LANES : (k + 1) * LANES].astype(BF16)

        return 0

    lax.fori_loop(0, groups // NC, arrive, 0)
    reduce.step()
    lax.fori_loop(groups // NC, groups, arrive, 0)

    def keep(p, _):
        dr, dl = device(p // (NZ * slab), (p // slab) % NZ, (p // NX) % ny, p % NX)
        pltpu.make_async_copy(w.at[p], blocks_ref.at[dr * (NZ * NYL * NC) + dl], keep_sem).start()
        return 0

    lax.fori_loop(0, n, keep, 0)

    z_order = [d % NZ for d in range(1, NZ + 1)]
    for j in range(STEPS):
        done = []
        low = raw[...].astype(BF16)
        if j:
            right[j * B : (j + 1) * B, :] = raw[...]
            gram = dot(raw[...], right[0 : (j + 1) * B, :], NT)
            newest = image_ref[(j - 1) * B : j * B, :]
            reduce = Reduce(jnp.concatenate([gram, dot(newest, image_ref[0 : j * B, :], NT)], 1), j)

        core_copies = {}
        for d in z_order:
            def put(i, value, d=d):
                core_out[d, i] = value.astype(BF16)
            if j:
                product_slab(low, base_of(1 - core, (z + d) % NZ), put)
            core_copies[d] = swap(core_out.at[d], core_in.at[j, d], j, RSC, d)
        if j:
            reduce.step()
        flights = [[] for _ in STREAMS]

        def first(t, d):
            axis = STREAMS[t][2][0]
            flights[t].append(send(out1[t].at[(here[axis] + d) % sizes[axis]], in1[t].at[j, d - 1],
                                   j, RS + t, d, axis))

        for d in z_order:
            core_copies[d].wait_recv()
            at = {"z": (z + d) % NZ}

            def put(i, value, d=d, at=at):
                value = value + core_in[j, d, i].astype(F32)
                at = {"z": at["z"], "y": i // NX, "x": i % NX}
                acc[at["z"] * slab + i] = value
                for t, (lo, hi, (p, q, r)) in enumerate(STREAMS):
                    out1[t][at[p], at[q] * sizes[r] + at[r]] = value[lo:hi].astype(BF16)

            if j:
                product_slab(low, base_of(core, at["z"]), put)
            else:
                for i in range(slab):
                    put(i, acc[at["z"] * slab + i])
            if d:
                first(0, d)
        for t in (1, 2):
            for d in range(1, sizes[STREAMS[t][2][0]]):
                first(t, d)
        done += list(core_copies.values())
        reduce.step()
        second = [[] for _ in STREAMS]
        for t in (1, 2, 0):
            lo, hi, (p, q, r) = STREAMS[t]
            for copy in flights[t]:
                copy.wait_recv()

            def add(iq, _):
                for ir in range(sizes[r]):
                    at = {p: here[p], q: iq, r: ir}
                    value = acc[(at["z"] * ny + at["y"]) * NX + at["x"], lo:hi]
                    for i in range(sizes[p] - 1):
                        value = value + in1[t][j, i, iq * sizes[r] + ir].astype(F32)
                    out2[t][iq, ir] = value
                return 0

            lax.fori_loop(0, sizes[q], add, 0)
            for d in range(1, sizes[q]):
                second[t].append(send(out2[t].at[(here[q] + d) % sizes[q]], in2[t].at[j, d - 1],
                                      j, RS + 3 + t, d, q))
            done += flights[t]
        reduce.step()
        third = [[] for _ in STREAMS]
        for t in (1, 2, 0):
            lo, hi, (p, q, r) = STREAMS[t]
            for copy in second[t]:
                copy.wait_recv()
            for ir in range(sizes[r]):
                value = out2[t][here[q], ir]
                for i in range(sizes[q] - 1):
                    value = value + in2[t][j, i, ir]
                out3[t][ir] = value
            for d in range(1, sizes[r]):
                third[t].append(send(out3[t].at[(here[r] + d) % sizes[r]], in3[t].at[j, d - 1],
                                     j, RS + 6 + t, d, r))
            done += second[t]
        reduce.step()
        total = reduce.step()
        done += reduce.sent

        cross = total[:, 0 : j * B]
        clean = total[:, j * B : (j + 1) * B]
        if j:
            gram_ref[(j - 1) * B : j * B, 0 : j * B] = total[:, (j + 1) * B : (2 * j + 1) * B]
            clean = clean - dot(cross, cross, NT)
        solve = inverse_factor(clean)

        parts = []
        for t in range(len(STREAMS)):
            lo, hi, (p, q, r) = STREAMS[t]
            value = out3[t][here[r]]
            for i, copy in enumerate(third[t]):
                copy.wait_recv()
                value = value + in3[t][j, i]
            parts.append(value)
            done += third[t]
        mine = jnp.concatenate(parts, 0)
        if j:
            mine = mine - dot(cross, own[0 : j * B, :])
        mine = dot(solve, mine)
        own[j * B : (j + 1) * B, :] = mine

        gathered[j, core, z, y, x] = mine.astype(BF16)

        def spread(t, phase):
            lo, hi, (p, q, r) = STREAMS[t]
            axis = (r, q, p)[phase]
            free = ("", r, r + q)[phase]
            at = [pl.ds(0, sizes[a]) if a in free else here[a] for a in "zyx"]
            piece = gathered.at[j, core, at[0], at[1], at[2], pl.ds(lo, hi - lo)]
            return [send(piece, piece, j, AG + 3 * phase + t, d, axis) for d in range(1, sizes[axis])]

        flights = [spread(t, 0) for t in range(len(STREAMS))]
        block = raw[...]
        if j:
            block = block - dot(cross, right[0 : j * B, :])
        right[j * B : (j + 1) * B, :] = dot(solve, block)
        for phase in (1, 2):
            for t in (0, 1, 2):
                for copy in flights[t]:
                    copy.wait_recv()
                done += flights[t]
                flights[t] = spread(t, phase)
        for t in (1, 2, 0):
            for copy in flights[t]:
                copy.wait_recv()
            done += flights[t]
        handed = []
        for d in range(NZ):
            piece = gathered.at[j, core, (z + d) % NZ]
            handed.append(swap(piece, piece, j, AGC, d))
        done += handed

        def back_slab(total, c, zz):
            wide = [jnp.concatenate([w[base_of(c, zz) + i] for i in range(slab)], 1)]
            for k in range(j + 1):
                wide.append(jnp.concatenate([gathered[k, c, zz, i // NX, i % NX] for i in range(slab)], 1))
            return total + fast(wide[-1], jnp.concatenate(wide, 0), NT)

        total = jnp.zeros((B, COLS + (j + 1) * B), F32)
        total = lax.fori_loop(0, NZ, lambda zz, total: back_slab(total, core, zz), total)

        def handed_in(d, total):
            piece = gathered.at[j, core, (z + d) % NZ]
            pltpu.make_async_remote_copy(
                src_ref=piece, dst_ref=piece, send_sem=send_sem.at[j, AGC, d], recv_sem=recv_sem.at[j, AGC, d],
                device_id=peer("c", 1), device_id_type=MESH).wait_recv()
            return back_slab(total, 1 - core, (z + d) % NZ)

        total = lax.fori_loop(0, NZ, handed_in, total)
        image, grams = total[:, :COLS], total[:, COLS:]

        clean = grams[:, j * B :]
        if j:
            table = coef_ref[0 : j * B, 0 : j * B]
            cross = dot(grams[:, : j * B], table, NT)
            clean = clean - dot(cross, cross, NT)
        solve = inverse_factor(clean)
        if j:
            image = image - dot(cross, image_ref[0 : j * B, :])
        image = dot(solve, image)
        image_ref[j * B : (j + 1) * B, :] = image
        if j + 1 < STEPS:
            raw[...] = image - dot(dot(solve, clean), right[j * B : (j + 1) * B, :])
        left = mine
        if j:
            left = left - dot(cross, left_ref[0 : j * B, :])
            coef_ref[j * B : (j + 1) * B, 0 : j * B] = -dot(solve, dot(cross, table))
        left_ref[j * B : (j + 1) * B, :] = dot(solve, left)
        coef_ref[j * B : (j + 1) * B, j * B : (j + 1) * B] = solve
        for copy in done:
            copy.wait_send()

    reduce = Reduce(dot(image_ref[(STEPS - 1) * B :, :], image_ref[...], NT), STEPS)
    total = None
    while total is None:
        total = reduce.step()
    gram_ref[(STEPS - 1) * B :, :] = total
    for copy in reduce.sent:
        copy.wait_send()
    pltpu.make_async_copy(w, blocks_ref, keep_sem).wait()


def chain(start_t, weight):
    ny = NYH * NYL
    slab = ny * NX
    n = NC * NZ * slab
    vmem = pl.BlockSpec(memory_space=pltpu.VMEM)
    hbm = pl.BlockSpec(memory_space=pl.ANY)
    s = STEPS * B
    sizes = {"z": NZ, "y": ny, "x": NX}

    def buffers(shape, kind):
        return [pltpu.VMEM(shape(*(sizes[a] for a in axes)) + (hi - lo, LANES), kind) for lo, hi, axes in STREAMS]

    return pl.pallas_call(
        chain_kernel,
        out_shape=(
            jax.ShapeDtypeStruct((STEPS, NC, NZ, ny, NX, B, LANES), BF16),
            jax.ShapeDtypeStruct((s, LANES), F32),
            jax.ShapeDtypeStruct((s, COLS), F32),
            jax.ShapeDtypeStruct((s, s), F32),
            jax.ShapeDtypeStruct((s, s), F32),
            jax.ShapeDtypeStruct((n, COLS, LANES), BF16),
        ),
        in_specs=[vmem, hbm],
        out_specs=[vmem] * 5 + [hbm],
        scratch_shapes=[
            pltpu.VMEM((n, COLS, LANES), BF16),
            pltpu.VMEM((2, ROWS, NX * COLS), BF16),
            pltpu.VMEM((n // NX, NX, SENT, LANES), BF16),
            pltpu.VMEM((NZ, slab, B, LANES), BF16),
            pltpu.VMEM((STEPS, NZ, slab, B, LANES), BF16),
            buffers(lambda p, q, r: (p, q * r), BF16),
            buffers(lambda p, q, r: (STEPS, max(p - 1, 1), q * r), BF16),
            buffers(lambda p, q, r: (q, r), F32),
            buffers(lambda p, q, r: (STEPS, max(q - 1, 1), r), F32),
            buffers(lambda p, q, r: (r,), F32),
            buffers(lambda p, q, r: (STEPS, max(r - 1, 1)), F32),
            pltpu.VMEM((NZ * slab, B, LANES), F32),
            pltpu.VMEM((STEPS + 1, 4, B, 3 * LANES), F32),
            pltpu.VMEM((STEPS + 1, 5, 3, B, 3 * LANES), F32),
            pltpu.VMEM((s, COLS), F32),
            pltpu.VMEM((B, COLS), F32),
            pltpu.VMEM((s, LANES), F32),
            pltpu.SemaphoreType.DMA((2,)),
            pltpu.SemaphoreType.DMA,
            pltpu.SemaphoreType.DMA((n // NX, NX)),
            pltpu.SemaphoreType.DMA((n // NX, NX)),
            pltpu.SemaphoreType.DMA((STEPS + 1, EXCHANGES, 4)),
            pltpu.SemaphoreType.DMA((STEPS + 1, EXCHANGES, 4)),
        ],
        compiler_params=pltpu.CompilerParams(
            collective_id=0, has_side_effects=True, vmem_limit_bytes=62 * 1024 * 1024),
    )(start_t, weight)


def sweep_kernel(gram_ref, coef_ref, left_ref, image_ref, adapter_left, adapter_right, low_right, high_ref, low_ref):
    g = [[None] * STEPS for _ in range(STEPS)]
    for i in range(STEPS):
        for k in range(i + 1):
            g[i][k] = gram_ref[i * B : (i + 1) * B, k * B : (k + 1) * B]
            if k < i:
                g[k][i] = g[i][k].T
    whole = jnp.concatenate([jnp.concatenate(r, 1) for r in g], 0)

    def orth(grown):
        top, bottom = grown[:B], grown[B:]
        one = inverse_factor(dot(top, top, NT))
        first = dot(one, top)
        cross = dot(bottom, first, NT)
        clean = bottom - dot(cross, first)
        two = inverse_factor(dot(clean, clean, NT))
        return jnp.concatenate([first, dot(two, clean)], 0)

    basis = orth(whole[:RANK])
    basis = lax.fori_loop(1, SWEEPS, lambda _, basis: orth(dot(basis, whole)), basis)
    adapter_left[...] = dot(basis, left_ref[...]).T[:ROWS]
    wide = dot(basis, image_ref[...]).T
    adapter_right[...] = wide
    low_right[...] = wide.astype(BF16)
    mixed = dot(basis, coef_ref[...])
    high = mixed.astype(BF16)
    high_ref[...] = high
    low_ref[...] = (mixed - high.astype(F32)).astype(BF16)


def sweeps(gram, coef, left, images):
    s = STEPS * B
    return pl.pallas_call(
        sweep_kernel,
        out_shape=(
            jax.ShapeDtypeStruct((ROWS, RANK), F32),
            jax.ShapeDtypeStruct((COLS, RANK), F32),
            jax.ShapeDtypeStruct((COLS, RANK), BF16),
            jax.ShapeDtypeStruct((RANK, s), BF16),
            jax.ShapeDtypeStruct((RANK, s), BF16),
        ),
    )(gram, coef, left, images)


PER = 8


def residual_kernel(gathered, high, low, right, weight, out):
    first = pl.program_id(0) * PER
    pieces = []
    for i in range(PER):
        at = first + i
        r, c = at // (NZ * NYL * NC), at % (NZ * NYL * NC)
        place = (c % NC, c // (NYL * NC), (r // NX) * NYL + (c // NC) % NYL, r % NX)
        pieces.append(jnp.concatenate([gathered[(k,) + place] for k in range(STEPS)], 0))
    stacked = jnp.concatenate(pieces, 1)
    left = (fast(high[...], stacked) + fast(low[...], stacked)).astype(BF16).T
    left = jnp.concatenate([left[i * LANES : i * LANES + ROWS] for i in range(PER)], 0)
    update = fast(right[...], left, NT)
    lane = lax.broadcasted_iota(jnp.int32, (COLS, LANES), 1)
    gap = LANES - ROWS
    for t in range(PER * ROWS // LANES):
        block = weight[t].astype(F32)
        if t:
            block = pltpu.roll(block, LANES - gap * t, 1)
        after = pltpu.roll(weight[t + 1].astype(F32), ROWS - gap * t, 1)
        block = jnp.where(lane < ROWS - gap * t, block, after)
        at = slice(t * LANES, (t + 1) * LANES)
        out[:, at] = (block - update[:, at]).astype(BF16)


def residual(gathered, high, low, right, blocks):
    n = blocks.shape[0]
    whole = lambda a: pl.BlockSpec(a.shape, lambda i: (0,) * a.ndim)
    return pl.pallas_call(
        residual_kernel,
        grid=(n // PER,),
        out_shape=jax.ShapeDtypeStruct((COLS, n * ROWS), BF16),
        in_specs=[whole(gathered), whole(high), whole(low), whole(right),
                  pl.BlockSpec((PER, COLS, LANES), lambda i: (i, 0, 0))],
        out_specs=pl.BlockSpec((COLS, PER * ROWS), lambda i: (0, i)),
        compiler_params=pltpu.CompilerParams(vmem_limit_bytes=48 * 1024 * 1024),
    )(gathered, high, low, right, blocks)


def shards(weight, start):
    gathered, left, images, gram, coef, blocks = chain(start.T, weight)
    adapter_left, adapter_right, low_right, high, low = sweeps(gram, coef, left, images)
    out = residual(gathered, high, low, low_right, blocks)
    return (adapter_left, adapter_right, out.T)


def solution(mesh):
    return jax.shard_map(
        shards,
        mesh=mesh,
        in_specs=(P(("row", "col"), None), P(("col", "row"), None)),
        out_specs=(P(("row", "col"), None), P(("col", "row"), None), P(None, ("col", "row"))),
        check_vma=False,
    )
```

```python
import functools

import jax
import jax.numpy as jnp
from jax import lax
from jax.experimental import pallas as pl
from jax.experimental.pallas import tpu as pltpu
from jax.sharding import PartitionSpec as P

STEPS = 3
RANK = 128
PER = 8
SWEEPS = 4
B = 64
LANES = 128

NX, NYH, NYL, NZ, NC = 4, 2, 2, 4, 2
ROWS, COLS = 112, 416
GAP, TAIL = LANES - ROWS, 48
SENT = COLS - TAIL

HIGHEST = lax.Precision.HIGHEST
MESH = pl.DeviceIdType.MESH
F32 = jnp.float32
BF16 = jnp.bfloat16
NT = (((1,), (1,)), ((), ()))
NN = (((1,), (0,)), ((), ()))

STREAMS = ((0, 32, "zyx"), (32, 48, "yxz"), (48, 64, "xzy"))
RSC, RS, AG, AGC, ARC, ARZ, ARY, ARX, ARB = 0, 1, 10, 19, 20, 21, 22, 23, 24
EXCHANGES = 25


def dot(left, right, dims=NN):
    return lax.dot_general(left, right, dims, precision=HIGHEST, preferred_element_type=F32)


def fast(left, right, dims=NN):
    return lax.dot_general(left, right, dims, preferred_element_type=F32)


def inverse_factor(gram):
    sub = lax.broadcasted_iota(jnp.int32, (8, LANES), 0)
    lane = lax.broadcasted_iota(jnp.int32, (8, LANES), 1)
    wide = jnp.concatenate([gram, jnp.zeros_like(gram)], 1)
    n = B // 8
    rows = [jnp.where(lane == sub + (B + 8 * q), 1.0, wide[8 * q : 8 * q + 8]) for q in range(n)]
    for p in range(n):
        columns = {q: [jnp.broadcast_to(rows[q][:, 8 * p + k : 8 * p + k + 1], (8, LANES)) for k in range(8)]
                   for q in range(p, n)}
        scale = jnp.ones((8, LANES), F32)
        for k in range(8):
            pivot = columns[p][k][k : k + 1]
            inverse = 1.0 / pivot
            scale = jnp.where(sub == k, lax.rsqrt(pivot), scale)
            row = rows[p][k : k + 1] * inverse
            ahead = {i: columns[p][i][k : k + 1] * inverse for i in range(k + 1, 8)}
            for q in range(p, n):
                factor = columns[q][k]
                if q == p:
                    factor = jnp.where(sub > k, factor, 0.0)
                rows[q] = rows[q] - factor * row
                for i in range(k + 1, 8):
                    columns[q][i] = columns[q][i] - factor * ahead[i]
        rows[p] = rows[p] * scale
    return jnp.concatenate(rows, 0)[:, B:]


def pack(block):
    tail = block[SENT:].astype(F32)
    lane = lax.broadcasted_iota(jnp.int32, (TAIL, LANES), 1)
    pieces = []
    for m in range(ROWS // GAP):
        moved = pltpu.roll(tail, ROWS - GAP * m, 1)
        pieces.append(jnp.where(lane < ROWS, block[TAIL * m : TAIL * (m + 1)].astype(F32), moved).astype(BF16))
    return jnp.concatenate(pieces + [block[TAIL * (ROWS // GAP) : SENT]], 0)


def unpack(w, p):
    lane = lax.broadcasted_iota(jnp.int32, (TAIL, LANES), 1)
    tail = jnp.zeros((TAIL, LANES), F32)
    for m in range(ROWS // GAP):
        at = slice(TAIL * m, TAIL * (m + 1))
        piece = w[p, at].astype(F32)
        moved = pltpu.roll(piece, (LANES - ROWS + GAP * m) % LANES, 1)
        tail = jnp.where((lane >= GAP * m) & (lane < GAP * (m + 1)), moved, tail)
        w[p, at] = jnp.where(lane < ROWS, piece, 0.0).astype(BF16)
    w[p, SENT:] = tail.astype(BF16)


def chain_kernel(start_ref, weight_ref, gathered, left_ref, image_ref, gram_ref, coef_ref, blocks_ref,
                 w, strip, staged, core_out, core_in, out1, in1, out2, in2, out3, in3, acc,
                 ar_out, ar_in, right, raw, own, joined, join_sem, strip_sem, keep_sem, put_sem, get_sem, send_sem, recv_sem):
    ny = NYH * NYL
    slab = ny * NX
    n = NC * NZ * slab
    row_id = lax.axis_index("row")
    col_id = lax.axis_index("col")
    y_hi, x = row_id // NX, row_id % NX
    z, y_lo, core = col_id // (NYL * NC), (col_id // NC) % NYL, col_id % NC
    y = y_hi * NYL + y_lo
    here = {"z": z, "y": y, "x": x}
    sizes = {"c": NC, "z": NZ, "y": ny, "x": NX}

    def device(core, z, y, x):
        return ((y // NYL) * NX + x, (z * NYL + y % NYL) * NC + core)

    def spot(core, z, y, x):
        return ((core * NZ + z) * ny + y) * NX + x

    def peer(axis, d):
        if axis == "c":
            return device((core + d) % NC, z, y, x)
        if axis == "z":
            return device(core, (z + d) % NZ, y, x)
        if axis == "y":
            return device(core, z, (y + d) % ny, x)
        return device(core, z, y, (x + d) % NX)

    place = spot(core, z, y, x)

    groups = n // NX

    def offset(i):
        step, g = i // ny, i % ny
        return step // NZ, (g + step % NZ) % NZ, g

    def strip_copy(i):
        dc, dz, dy = offset(i)
        dr, dl = device((core + dc) % NC, (z + dz) % NZ, (y + dy) % ny, 0)
        block = dl * (NYH * NX) + dr
        return pltpu.make_async_copy(
            weight_ref.at[:, pl.ds(pl.multiple_of(block * COLS, LANES), NX * COLS)], strip.at[i % 2],
            strip_sem.at[i % 2])

    def block_copy(i, dx):
        dc, dz, dy = offset(i)
        tx = (x + dx) % NX
        return pltpu.make_async_remote_copy(
            src_ref=staged.at[i, tx], dst_ref=w.at[place, pl.ds(0, SENT)], send_sem=put_sem.at[i, dx], recv_sem=get_sem.at[i, dx],
            device_id=device((core + dc) % NC, (z + dz) % NZ, (y + dy) % ny, tx), device_id_type=MESH)

    strip_copy(0).start()
    barrier = pltpu.get_barrier_semaphore()

    def greet(d, _):
        to = (place + d) % n
        target = device(to // (NZ * slab), (to // slab) % NZ, (to // NX) % ny, to % NX)
        pl.semaphore_signal(barrier, inc=1, device_id=target, device_id_type=MESH)
        return 0

    lax.fori_loop(1, n, greet, 0)

    def stage(i):
        strip_copy(i).wait()

        @pl.when(i < groups - 1)
        def _():
            strip_copy(i + 1).start()

        value = strip[i % 2]
        value = jnp.concatenate([value, jnp.zeros((LANES - ROWS, NX * COLS), BF16)], 0).T
        for k in range(NX):
            staged[i, k] = pack(value[k * COLS : (k + 1) * COLS])

    def scatter(step, _):
        def each(g, _):
            stage(step * ny + g)
            return 0

        lax.fori_loop(0, ny, each, 0)

        @pl.when(step == 0)
        def _():
            pl.semaphore_wait(barrier, n - 1)
            pltpu.make_async_copy(staged.at[0, x], w.at[place, pl.ds(0, SENT)], keep_sem).start()

        def rotate(a, _):
            for dx in range(NX):
                i = step * ny + (dx + a) % ny
                if dx == 0:
                    @pl.when(i != 0)
                    def _():
                        block_copy(i, dx).start()
                else:
                    block_copy(i, dx).start()
            return 0

        lax.fori_loop(0, ny, rotate, 0)
        return 0

    lax.fori_loop(0, groups // ny, scatter, 0)

    def send_to(target, src, dst, j, phase, d):
        copy = pltpu.make_async_remote_copy(
            src_ref=src, dst_ref=dst, send_sem=send_sem.at[j, phase, d], recv_sem=recv_sem.at[j, phase, d],
            device_id=target, device_id_type=MESH)
        copy.start()
        return copy

    def send(src, dst, j, phase, d, axis):
        return send_to(peer(axis, d), src, dst, j, phase, d)

    def swap(src, dst, j, phase, d):
        return send_to(peer("c", 1), src, dst, j, phase, d)

    half = B // NC
    others = {"z": ARZ, "y": ARY, "x": ARX}

    class Reduce:
        def __init__(self, value, j):
            self.j, self.lanes, self.stage = j, value.shape[1], 0
            self.sent = []
            pad = -self.lanes % LANES
            if pad:
                value = jnp.concatenate([value, jnp.zeros((B, pad), F32)], 1)
            self.width = value.shape[1]
            out = ar_out.at[j, 0]
            out[:, : self.width] = value
            mine = pl.ds(pl.multiple_of(core * half, half), half)
            theirs = pl.ds(pl.multiple_of((1 - core) * half, half), half)
            self.mine = mine
            self.pending = [send(ar_out.at[j, 0, theirs, pl.ds(0, self.width)],
                                 ar_in.at[j, 0, 0, pl.ds(0, half), pl.ds(0, self.width)], j, ARC, 1, "c")]
            self.own = out[mine, : self.width]

        def step(self):
            j, width, s = self.j, self.width, self.stage
            total = self.own
            for i, copy in enumerate(self.pending):
                copy.wait_recv()
                if s < 4:
                    total = total + ar_in[j, s, i, 0:half, 0:width]
            self.sent += self.pending
            self.pending = []
            self.stage += 1
            if s < 3:
                axis = "zyx"[s]
                self.own = total
                ar_out[j, s + 1, 0:half, 0:width] = total
                for d in range(1, sizes[axis]):
                    self.pending.append(send(
                        ar_out.at[j, s + 1, pl.ds(0, half), pl.ds(0, width)],
                        ar_in.at[j, s + 1, d - 1, pl.ds(0, half), pl.ds(0, width)], j, others[axis], d, axis))
            elif s == 3:
                ar_in[j, 4, 0, self.mine, 0:width] = total
                there = ar_in.at[j, 4, 0, self.mine, pl.ds(0, width)]
                self.pending.append(send(there, there, j, ARB, 1, "c"))
            else:
                return ar_in[j, 4, 0, :, 0 : self.lanes]
            return None

    def product_slab(low, base, put):
        out = fast(low, jnp.concatenate([w[base + i] for i in range(slab)], 1))
        for i in range(slab):
            put(i, out[:, i * LANES : (i + 1) * LANES])

    def base_of(c, zz):
        return (c * NZ + zz) * slab

    raw[...] = start_ref[...]
    coef_ref[...] = jnp.zeros_like(coef_ref)
    start_low = raw[...].astype(BF16)
    right[0:B, :] = raw[...]
    reduce = Reduce(dot(raw[...], raw[...], NT), 0)
    pltpu.make_async_copy(staged.at[0, x], w.at[place, pl.ds(0, SENT)], keep_sem).wait()

    def arrive(i, _):
        dc, dz, dy = offset(i)
        fz, fy = (z - dz + NZ) % NZ, (y - dy + ny) % ny
        base = spot((core - dc + NC) % NC, fz, fy, 0)
        for dx in range(NX):
            if dx == 0:
                @pl.when(i != 0)
                def _():
                    block_copy(i, dx).wait()
            else:
                block_copy(i, dx).wait()
        for k in range(NX):
            unpack(w, base + k)
        out = fast(start_low, jnp.concatenate([w[base + k] for k in range(NX)], 1))

        @pl.when(dc == 0)
        def _():
            for k in range(NX):
                acc[(fz * ny + fy) * NX + k] = out[:, k * LANES : (k + 1) * LANES]

        @pl.when(dc != 0)
        def _():
            for k in range(NX):
                core_out[(NZ - dz) % NZ, fy * NX + k] = out[:, k * LANES : (k + 1) * LANES].astype(BF16)

        return 0

    lax.fori_loop(0, groups // NC, arrive, 0)
    reduce.step()
    lax.fori_loop(groups // NC, groups, arrive, 0)

    lane = lax.broadcasted_iota(jnp.int32, (COLS, LANES), 1)
    spans = n // PER

    def joined_copy(i):
        return pltpu.make_async_copy(
            joined.at[i % 2], blocks_ref.at[:, pl.ds(pl.multiple_of(i * PER * ROWS, LANES), PER * ROWS)],
            join_sem.at[i % 2])

    def join(i, _):
        @pl.when(i >= 2)
        def _():
            joined_copy(i - 2).wait()

        parts = []
        for k in range(PER):
            at = i * PER + k
            r, c = at // (NZ * NYL * NC), at % (NZ * NYL * NC)
            parts.append(spot(c % NC, c // (NYL * NC), (r // NX) * NYL + (c // NC) % NYL, r % NX))
        for t in range(PER * ROWS // LANES):
            first = w[parts[t]].astype(F32)
            if t:
                first = pltpu.roll(first, LANES - GAP * t, 1)
            after = pltpu.roll(w[parts[t + 1]].astype(F32), ROWS - GAP * t, 1)
            joined[i % 2, :, t * LANES : (t + 1) * LANES] = jnp.where(lane < ROWS - GAP * t, first, after).astype(BF16)
        joined_copy(i).start()
        return 0

    quota = iter([(i * spans // (2 * STEPS), (i + 1) * spans // (2 * STEPS)) for i in range(2 * STEPS)])

    def fill():
        lo, hi = next(quota)
        lax.fori_loop(lo, hi, join, 0)

    z_order = [d % NZ for d in range(1, NZ + 1)]
    for j in range(STEPS):
        done = []
        low = raw[...].astype(BF16)
        if j:
            right[j * B : (j + 1) * B, :] = raw[...]
            gram = dot(raw[...], right[0 : (j + 1) * B, :], NT)
            newest = image_ref[(j - 1) * B : j * B, :]
            reduce = Reduce(jnp.concatenate([gram, dot(newest, image_ref[0 : j * B, :], NT)], 1), j)

        core_copies = {}
        for d in z_order:
            def put(i, value, d=d):
                core_out[d, i] = value.astype(BF16)
            if j:
                product_slab(low, base_of(1 - core, (z + d) % NZ), put)
            core_copies[d] = swap(core_out.at[d], core_in.at[j, d], j, RSC, d)
        if j:
            reduce.step()
        flights = [[] for _ in STREAMS]

        def first(t, d):
            axis = STREAMS[t][2][0]
            flights[t].append(send(out1[t].at[(here[axis] + d) % sizes[axis]], in1[t].at[j, d - 1],
                                   j, RS + t, d, axis))

        for d in z_order:
            core_copies[d].wait_recv()
            at = {"z": (z + d) % NZ}

            def put(i, value, d=d, at=at):
                value = value + core_in[j, d, i].astype(F32)
                at = {"z": at["z"], "y": i // NX, "x": i % NX}
                acc[at["z"] * slab + i] = value
                for t, (lo, hi, (p, q, r)) in enumerate(STREAMS):
                    out1[t][at[p], at[q] * sizes[r] + at[r]] = value[lo:hi].astype(BF16)

            if j:
                product_slab(low, base_of(core, at["z"]), put)
            else:
                for i in range(slab):
                    put(i, acc[at["z"] * slab + i])
            if d:
                first(0, d)
        for t in (1, 2):
            for d in range(1, sizes[STREAMS[t][2][0]]):
                first(t, d)
        done += list(core_copies.values())
        reduce.step()
        fill()
        reduce.step()
        second = [[] for _ in STREAMS]
        for t in (1, 2, 0):
            lo, hi, (p, q, r) = STREAMS[t]
            for copy in flights[t]:
                copy.wait_recv()

            def add(iq, _):
                for ir in range(sizes[r]):
                    at = {p: here[p], q: iq, r: ir}
                    value = acc[(at["z"] * ny + at["y"]) * NX + at["x"], lo:hi]
                    for i in range(sizes[p] - 1):
                        value = value + in1[t][j, i, iq * sizes[r] + ir].astype(F32)
                    out2[t][iq, ir] = value
                return 0

            lax.fori_loop(0, sizes[q], add, 0)
            for d in range(1, sizes[q]):
                second[t].append(send(out2[t].at[(here[q] + d) % sizes[q]], in2[t].at[j, d - 1],
                                      j, RS + 3 + t, d, q))
            done += flights[t]
        reduce.step()
        third = [[] for _ in STREAMS]
        for t in (1, 2, 0):
            lo, hi, (p, q, r) = STREAMS[t]
            for copy in second[t]:
                copy.wait_recv()
            for ir in range(sizes[r]):
                value = out2[t][here[q], ir]
                for i in range(sizes[q] - 1):
                    value = value + in2[t][j, i, ir]
                out3[t][ir] = value
            for d in range(1, sizes[r]):
                third[t].append(send(out3[t].at[(here[r] + d) % sizes[r]], in3[t].at[j, d - 1],
                                     j, RS + 6 + t, d, r))
            done += second[t]
        total = reduce.step()
        done += reduce.sent

        cross = total[:, 0 : j * B]
        clean = total[:, j * B : (j + 1) * B]
        if j:
            gram_ref[(j - 1) * B : j * B, 0 : j * B] = total[:, (j + 1) * B : (2 * j + 1) * B]
            clean = clean - dot(cross, cross, NT)
        solve = inverse_factor(clean)

        parts = []
        for t in range(len(STREAMS)):
            lo, hi, (p, q, r) = STREAMS[t]
            value = out3[t][here[r]]
            for i, copy in enumerate(third[t]):
                copy.wait_recv()
                value = value + in3[t][j, i]
            parts.append(value)
            done += third[t]
        mine = jnp.concatenate(parts, 0)
        if j:
            mine = mine - dot(cross, own[0 : j * B, :])
        mine = dot(solve, mine)
        own[j * B : (j + 1) * B, :] = mine

        gathered[j, core, z, y, x] = mine.astype(BF16)

        def spread(t, phase):
            lo, hi, (p, q, r) = STREAMS[t]
            axis = (r, q, p)[phase]
            free = ("", r, r + q)[phase]
            at = [pl.ds(0, sizes[a]) if a in free else here[a] for a in "zyx"]
            piece = gathered.at[j, core, at[0], at[1], at[2], pl.ds(lo, hi - lo)]
            return [send(piece, piece, j, AG + 3 * phase + t, d, axis) for d in range(1, sizes[axis])]

        flights = [spread(t, 0) for t in range(len(STREAMS))]
        block = raw[...]
        if j:
            block = block - dot(cross, right[0 : j * B, :])
        right[j * B : (j + 1) * B, :] = dot(solve, block)
        for phase in (1, 2):
            for t in (0, 1, 2):
                for copy in flights[t]:
                    copy.wait_recv()
                done += flights[t]
                flights[t] = spread(t, phase)
        fill()
        for t in (1, 2, 0):
            for copy in flights[t]:
                copy.wait_recv()
            done += flights[t]
        handed = []
        for d in range(NZ):
            piece = gathered.at[j, core, (z + d) % NZ]
            handed.append(swap(piece, piece, j, AGC, d))
        done += handed

        def back_slab(total, c, zz):
            wide = [jnp.concatenate([w[base_of(c, zz) + i] for i in range(slab)], 1)]
            for k in range(j + 1):
                wide.append(jnp.concatenate([gathered[k, c, zz, i // NX, i % NX] for i in range(slab)], 1))
            return total + fast(wide[-1], jnp.concatenate(wide, 0), NT)

        total = jnp.zeros((B, COLS + (j + 1) * B), F32)
        total = lax.fori_loop(0, NZ, lambda zz, total: back_slab(total, core, zz), total)

        def handed_in(d, total):
            piece = gathered.at[j, core, (z + d) % NZ]
            pltpu.make_async_remote_copy(
                src_ref=piece, dst_ref=piece, send_sem=send_sem.at[j, AGC, d], recv_sem=recv_sem.at[j, AGC, d],
                device_id=peer("c", 1), device_id_type=MESH).wait_recv()
            return back_slab(total, 1 - core, (z + d) % NZ)

        total = lax.fori_loop(0, NZ, handed_in, total)
        image, grams = total[:, :COLS], total[:, COLS:]

        clean = grams[:, j * B :]
        if j:
            table = coef_ref[0 : j * B, 0 : j * B]
            cross = dot(grams[:, : j * B], table, NT)
            clean = clean - dot(cross, cross, NT)
        solve = inverse_factor(clean)
        if j:
            image = image - dot(cross, image_ref[0 : j * B, :])
        image = dot(solve, image)
        image_ref[j * B : (j + 1) * B, :] = image
        if j + 1 < STEPS:
            raw[...] = image - dot(dot(solve, clean), right[j * B : (j + 1) * B, :])
        left = mine
        if j:
            left = left - dot(cross, left_ref[0 : j * B, :])
            coef_ref[j * B : (j + 1) * B, 0 : j * B] = -dot(solve, dot(cross, table))
        left_ref[j * B : (j + 1) * B, :] = dot(solve, left)
        coef_ref[j * B : (j + 1) * B, j * B : (j + 1) * B] = solve
        for copy in done:
            copy.wait_send()

    reduce = Reduce(dot(image_ref[(STEPS - 1) * B :, :], image_ref[...], NT), STEPS)
    total = None
    while total is None:
        total = reduce.step()
    gram_ref[(STEPS - 1) * B :, :] = total
    for copy in reduce.sent:
        copy.wait_send()
    joined_copy(spans - 2).wait()
    joined_copy(spans - 1).wait()


def chain(start_t, weight):
    ny = NYH * NYL
    slab = ny * NX
    n = NC * NZ * slab
    vmem = pl.BlockSpec(memory_space=pltpu.VMEM)
    hbm = pl.BlockSpec(memory_space=pl.ANY)
    s = STEPS * B
    sizes = {"z": NZ, "y": ny, "x": NX}

    def buffers(shape, kind):
        return [pltpu.VMEM(shape(*(sizes[a] for a in axes)) + (hi - lo, LANES), kind) for lo, hi, axes in STREAMS]

    return pl.pallas_call(
        chain_kernel,
        out_shape=(
            jax.ShapeDtypeStruct((STEPS, NC, NZ, ny, NX, B, LANES), BF16),
            jax.ShapeDtypeStruct((s, LANES), F32),
            jax.ShapeDtypeStruct((s, COLS), F32),
            jax.ShapeDtypeStruct((s, s), F32),
            jax.ShapeDtypeStruct((s, s), F32),
            jax.ShapeDtypeStruct((COLS, n * ROWS), BF16),
        ),
        in_specs=[vmem, hbm],
        out_specs=[vmem] * 5 + [hbm],
        scratch_shapes=[
            pltpu.VMEM((n, COLS, LANES), BF16),
            pltpu.VMEM((2, ROWS, NX * COLS), BF16),
            pltpu.VMEM((n // NX, NX, SENT, LANES), BF16),
            pltpu.VMEM((NZ, slab, B, LANES), BF16),
            pltpu.VMEM((STEPS, NZ, slab, B, LANES), BF16),
            buffers(lambda p, q, r: (p, q * r), BF16),
            buffers(lambda p, q, r: (STEPS, max(p - 1, 1), q * r), BF16),
            buffers(lambda p, q, r: (q, r), F32),
            buffers(lambda p, q, r: (STEPS, max(q - 1, 1), r), F32),
            buffers(lambda p, q, r: (r,), F32),
            buffers(lambda p, q, r: (STEPS, max(r - 1, 1)), F32),
            pltpu.VMEM((NZ * slab, B, LANES), F32),
            pltpu.VMEM((STEPS + 1, 4, B, 3 * LANES), F32),
            pltpu.VMEM((STEPS + 1, 5, 3, B, 3 * LANES), F32),
            pltpu.VMEM((s, COLS), F32),
            pltpu.VMEM((B, COLS), F32),
            pltpu.VMEM((s, LANES), F32),
            pltpu.VMEM((2, COLS, PER * ROWS), BF16),
            pltpu.SemaphoreType.DMA((2,)),
            pltpu.SemaphoreType.DMA((2,)),
            pltpu.SemaphoreType.DMA,
            pltpu.SemaphoreType.DMA((n // NX, NX)),
            pltpu.SemaphoreType.DMA((n // NX, NX)),
            pltpu.SemaphoreType.DMA((STEPS + 1, EXCHANGES, 4)),
            pltpu.SemaphoreType.DMA((STEPS + 1, EXCHANGES, 4)),
        ],
        compiler_params=pltpu.CompilerParams(
            collective_id=0, has_side_effects=True, vmem_limit_bytes=62 * 1024 * 1024),
    )(start_t, weight)


def sweeps(gram_ref, coef_ref):
    g = [[None] * STEPS for _ in range(STEPS)]
    for i in range(STEPS):
        for k in range(i + 1):
            g[i][k] = gram_ref[i * B : (i + 1) * B, k * B : (k + 1) * B]
            if k < i:
                g[k][i] = g[i][k].T
    whole = jnp.concatenate([jnp.concatenate(r, 1) for r in g], 0)

    def orth(grown):
        top, bottom = grown[:B], grown[B:]
        one = inverse_factor(dot(top, top, NT))
        first = dot(one, top)
        cross = dot(bottom, first, NT)
        clean = bottom - dot(cross, first)
        two = inverse_factor(dot(clean, clean, NT))
        return jnp.concatenate([first, dot(two, clean)], 0)

    basis = orth(whole[:RANK])
    return lax.fori_loop(1, SWEEPS, lambda _, basis: orth(dot(basis, whole)), basis)


def finish_kernel(gram_ref, coef_ref, left_ref, image_ref, gathered, weight,
                  adapter_left, adapter_right, out, high, low, right):
    @pl.when(pl.program_id(0) == 0)
    def _():
        basis = sweeps(gram_ref, coef_ref)
        adapter_left[...] = dot(basis, left_ref[...]).T[:ROWS]
        wide = dot(basis, image_ref[...]).T
        adapter_right[...] = wide
        right[...] = wide.astype(BF16)
        mixed = dot(basis, coef_ref[...])
        high[...] = mixed.astype(BF16)
        low[...] = (mixed - mixed.astype(BF16).astype(F32)).astype(BF16)

    pieces = []
    for i in range(PER):
        at = pl.program_id(0) * PER + i
        r, c = at // (NZ * NYL * NC), at % (NZ * NYL * NC)
        place = (c % NC, c // (NYL * NC), (r // NX) * NYL + (c // NC) % NYL, r % NX)
        pieces.append(jnp.concatenate([gathered[(k,) + place] for k in range(STEPS)], 0))
    stacked = jnp.concatenate(pieces, 1)
    left = (fast(high[...], stacked) + fast(low[...], stacked)).astype(BF16).T
    left = jnp.concatenate([left[i * LANES : i * LANES + ROWS] for i in range(PER)], 0)
    out[...] = (weight[...].astype(F32) - fast(right[...], left, NT)).astype(BF16)


def finish(gram, coef, left, images, gathered, blocks):
    rows = blocks.shape[1]
    s = STEPS * B
    whole = lambda shape: pl.BlockSpec(shape, lambda i: (0,) * len(shape))
    strip = pl.BlockSpec((COLS, PER * ROWS), lambda i: (0, i))
    return pl.pallas_call(
        finish_kernel,
        grid=(rows // (PER * ROWS),),
        out_shape=(
            jax.ShapeDtypeStruct((ROWS, RANK), F32),
            jax.ShapeDtypeStruct((COLS, RANK), F32),
            jax.ShapeDtypeStruct((COLS, rows), BF16),
        ),
        in_specs=[whole(a.shape) for a in (gram, coef, left, images, gathered)] + [strip],
        out_specs=(whole((ROWS, RANK)), whole((COLS, RANK)), strip),
        scratch_shapes=[pltpu.VMEM((RANK, s), BF16), pltpu.VMEM((RANK, s), BF16), pltpu.VMEM((COLS, RANK), BF16)],
        compiler_params=pltpu.CompilerParams(vmem_limit_bytes=48 * 1024 * 1024),
    )(gram, coef, left, images, gathered, blocks)


def shards(weight, start):
    gathered, left, images, gram, coef, blocks = chain(start.T, weight)
    adapter_left, adapter_right, out = finish(gram, coef, left, images, gathered, blocks)
    return (adapter_left, adapter_right, out.T)


def solution(mesh):
    return jax.shard_map(
        shards,
        mesh=mesh,
        in_specs=(P(("row", "col"), None), P(("col", "row"), None)),
        out_specs=(P(("row", "col"), None), P(("col", "row"), None), P(None, ("col", "row"))),
        check_vma=False,
    )
```

```python
import functools

import jax
import jax.numpy as jnp
from jax import lax
from jax.experimental import pallas as pl
from jax.experimental.pallas import tpu as pltpu
from jax.sharding import PartitionSpec as P

STEPS = 3
RANK = 128
PER = 8
SWEEPS = 4
B = 64
LANES = 128

NX, NYH, NYL, NZ, NC = 4, 2, 2, 4, 2
ROWS, COLS = 112, 416
GAP, TAIL = LANES - ROWS, 48
SENT = COLS - TAIL

HIGHEST = lax.Precision.HIGHEST
MESH = pl.DeviceIdType.MESH
F32 = jnp.float32
BF16 = jnp.bfloat16
NT = (((1,), (1,)), ((), ()))
NN = (((1,), (0,)), ((), ()))

STREAMS = ((0, 32, "zyx"), (32, 48, "yxz"), (48, 64, "xzy"))
RSC, RS, AG, AGC, ARC, ARZ, ARY, ARX, ARB = 0, 1, 10, 19, 20, 21, 22, 23, 24
EXCHANGES = 25


def labels(core, z, y, x):
    return z + core * (y - z), y + core * (x - y), x + core * (z - x)


def chip(core, a, b, c):
    return a + core * (c - a), b + core * (a - b), c + core * (b - c)


def dot(left, right, dims=NN):
    return lax.dot_general(left, right, dims, precision=HIGHEST, preferred_element_type=F32)


def fast(left, right, dims=NN):
    return lax.dot_general(left, right, dims, preferred_element_type=F32)


def inverse_factor(gram):
    sub = lax.broadcasted_iota(jnp.int32, (8, LANES), 0)
    lane = lax.broadcasted_iota(jnp.int32, (8, LANES), 1)
    wide = jnp.concatenate([gram, jnp.zeros_like(gram)], 1)
    n = B // 8
    rows = [jnp.where(lane == sub + (B + 8 * q), 1.0, wide[8 * q : 8 * q + 8]) for q in range(n)]
    for p in range(n):
        columns = {q: [jnp.broadcast_to(rows[q][:, 8 * p + k : 8 * p + k + 1], (8, LANES)) for k in range(8)]
                   for q in range(p, n)}
        scale = jnp.ones((8, LANES), F32)
        for k in range(8):
            pivot = columns[p][k][k : k + 1]
            inverse = 1.0 / pivot
            scale = jnp.where(sub == k, lax.rsqrt(pivot), scale)
            row = rows[p][k : k + 1] * inverse
            ahead = {i: columns[p][i][k : k + 1] * inverse for i in range(k + 1, 8)}
            for q in range(p, n):
                factor = columns[q][k]
                if q == p:
                    factor = jnp.where(sub > k, factor, 0.0)
                rows[q] = rows[q] - factor * row
                for i in range(k + 1, 8):
                    columns[q][i] = columns[q][i] - factor * ahead[i]
        rows[p] = rows[p] * scale
    return jnp.concatenate(rows, 0)[:, B:]


def pack(block):
    tail = block[SENT:].astype(F32)
    lane = lax.broadcasted_iota(jnp.int32, (TAIL, LANES), 1)
    pieces = []
    for m in range(ROWS // GAP):
        moved = pltpu.roll(tail, ROWS - GAP * m, 1)
        pieces.append(jnp.where(lane < ROWS, block[TAIL * m : TAIL * (m + 1)].astype(F32), moved).astype(BF16))
    return jnp.concatenate(pieces + [block[TAIL * (ROWS // GAP) : SENT]], 0)


def unpack(w, p):
    lane = lax.broadcasted_iota(jnp.int32, (TAIL, LANES), 1)
    tail = jnp.zeros((TAIL, LANES), F32)
    for m in range(ROWS // GAP):
        at = slice(TAIL * m, TAIL * (m + 1))
        piece = w[p, at].astype(F32)
        moved = pltpu.roll(piece, (LANES - ROWS + GAP * m) % LANES, 1)
        tail = jnp.where((lane >= GAP * m) & (lane < GAP * (m + 1)), moved, tail)
        w[p, at] = jnp.where(lane < ROWS, piece, 0.0).astype(BF16)
    w[p, SENT:] = tail.astype(BF16)


def chain_kernel(start_ref, weight_ref, gathered, left_ref, image_ref, gram_ref, coef_ref, blocks_ref,
                 w, strip, staged, core_out, core_in, out1, in1, out2, in2, out3, in3, acc,
                 ar_out, ar_in, right, raw, own, joined, join_sem, strip_sem, keep_sem, put_sem, get_sem, send_sem, recv_sem):
    ny = NYH * NYL
    slab = ny * NX
    n = NC * NZ * slab
    row_id = lax.axis_index("row")
    col_id = lax.axis_index("col")
    y_hi, x = row_id // NX, row_id % NX
    z, y_lo, core = col_id // (NYL * NC), (col_id // NC) % NYL, col_id % NC
    site = (z, y_hi * NYL + y_lo, x)
    z, y, x = labels(core, *site)
    partner_z = labels(1 - core, *site)[0]
    here = {"z": z, "y": y, "x": x}
    sizes = {"c": NC, "z": NZ, "y": ny, "x": NX}

    def device_at(core, z, y, x):
        return ((y // NYL) * NX + x, (z * NYL + y % NYL) * NC + core)

    def device(core, z, y, x):
        return device_at(core, *chip(core, z, y, x))

    def spot(core, z, y, x):
        return ((core * NZ + z) * ny + y) * NX + x

    def peer(axis, d):
        if axis == "c":
            return device_at((core + d) % NC, *site)
        if axis == "z":
            return device(core, (z + d) % NZ, y, x)
        if axis == "y":
            return device(core, z, (y + d) % ny, x)
        return device(core, z, y, (x + d) % NX)

    place = spot(core, z, y, x)

    groups = n // NX

    def offset(i):
        step, g = i // ny, i % ny
        return step // NZ, (g + step % NZ) % NZ, g

    def strip_copy(i):
        dc, dz, dy = offset(i)
        dr, dl = device_at((core + dc) % NC, (site[0] + dz) % NZ, (site[1] + dy) % ny, 0)
        block = dl * (NYH * NX) + dr
        return pltpu.make_async_copy(
            weight_ref.at[:, pl.ds(pl.multiple_of(block * COLS, LANES), NX * COLS)], strip.at[i % 2],
            strip_sem.at[i % 2])

    def block_copy(i, dx):
        dc, dz, dy = offset(i)
        tx = (site[2] + dx) % NX
        return pltpu.make_async_remote_copy(
            src_ref=staged.at[i, tx], dst_ref=w.at[place, pl.ds(0, SENT)], send_sem=put_sem.at[i, dx], recv_sem=get_sem.at[i, dx],
            device_id=device_at((core + dc) % NC, (site[0] + dz) % NZ, (site[1] + dy) % ny, tx), device_id_type=MESH)

    strip_copy(0).start()
    barrier = pltpu.get_barrier_semaphore()

    def greet(d, _):
        to = (place + d) % n
        target = device(to // (NZ * slab), (to // slab) % NZ, (to // NX) % ny, to % NX)
        pl.semaphore_signal(barrier, inc=1, device_id=target, device_id_type=MESH)
        return 0

    lax.fori_loop(1, n, greet, 0)

    def stage(i):
        strip_copy(i).wait()

        @pl.when(i < groups - 1)
        def _():
            strip_copy(i + 1).start()

        value = strip[i % 2]
        value = jnp.concatenate([value, jnp.zeros((LANES - ROWS, NX * COLS), BF16)], 0).T
        for k in range(NX):
            staged[i, k] = pack(value[k * COLS : (k + 1) * COLS])

    def scatter(step, _):
        def each(g, _):
            stage(step * ny + g)
            return 0

        lax.fori_loop(0, ny, each, 0)

        @pl.when(step == 0)
        def _():
            pl.semaphore_wait(barrier, n - 1)
            pltpu.make_async_copy(staged.at[0, site[2]], w.at[place, pl.ds(0, SENT)], keep_sem).start()

        def rotate(a, _):
            for dx in range(NX):
                i = step * ny + (dx + a) % ny
                if dx == 0:
                    @pl.when(i != 0)
                    def _():
                        block_copy(i, dx).start()
                else:
                    block_copy(i, dx).start()
            return 0

        lax.fori_loop(0, ny, rotate, 0)
        return 0

    lax.fori_loop(0, groups // ny, scatter, 0)

    def send_to(target, src, dst, j, phase, d):
        copy = pltpu.make_async_remote_copy(
            src_ref=src, dst_ref=dst, send_sem=send_sem.at[j, phase, d], recv_sem=recv_sem.at[j, phase, d],
            device_id=target, device_id_type=MESH)
        copy.start()
        return copy

    def send(src, dst, j, phase, d, axis):
        return send_to(peer(axis, d), src, dst, j, phase, d)

    def swap(src, dst, j, phase, d):
        return send_to(peer("c", 1), src, dst, j, phase, d)

    half = B // NC
    others = {"z": ARZ, "y": ARY, "x": ARX}

    class Reduce:
        def __init__(self, value, j):
            self.j, self.lanes, self.stage = j, value.shape[1], 0
            self.sent = []
            pad = -self.lanes % LANES
            if pad:
                value = jnp.concatenate([value, jnp.zeros((B, pad), F32)], 1)
            self.width = value.shape[1]
            out = ar_out.at[j, 0]
            out[:, : self.width] = value
            mine = pl.ds(pl.multiple_of(core * half, half), half)
            theirs = pl.ds(pl.multiple_of((1 - core) * half, half), half)
            self.mine = mine
            self.pending = [send(ar_out.at[j, 0, theirs, pl.ds(0, self.width)],
                                 ar_in.at[j, 0, 0, pl.ds(0, half), pl.ds(0, self.width)], j, ARC, 1, "c")]
            self.own = out[mine, : self.width]

        def step(self):
            j, width, s = self.j, self.width, self.stage
            total = self.own
            for i, copy in enumerate(self.pending):
                copy.wait_recv()
                if s < 4:
                    total = total + ar_in[j, s, i, 0:half, 0:width]
            self.sent += self.pending
            self.pending = []
            self.stage += 1
            if s < 3:
                axis = "zyx"[s]
                self.own = total
                ar_out[j, s + 1, 0:half, 0:width] = total
                for d in range(1, sizes[axis]):
                    self.pending.append(send(
                        ar_out.at[j, s + 1, pl.ds(0, half), pl.ds(0, width)],
                        ar_in.at[j, s + 1, d - 1, pl.ds(0, half), pl.ds(0, width)], j, others[axis], d, axis))
            elif s == 3:
                ar_in[j, 4, 0, self.mine, 0:width] = total
                there = ar_in.at[j, 4, 0, self.mine, pl.ds(0, width)]
                self.pending.append(send(there, there, j, ARB, 1, "c"))
            else:
                return ar_in[j, 4, 0, :, 0 : self.lanes]
            return None

    def product_slab(low, base, put):
        out = fast(low, jnp.concatenate([w[base + i] for i in range(slab)], 1))
        for i in range(slab):
            put(i, out[:, i * LANES : (i + 1) * LANES])

    def base_of(c, zz):
        return (c * NZ + zz) * slab

    raw[...] = start_ref[...]
    coef_ref[...] = jnp.zeros_like(coef_ref)
    start_low = raw[...].astype(BF16)
    right[0:B, :] = raw[...]
    reduce = Reduce(dot(raw[...], raw[...], NT), 0)
    pltpu.make_async_copy(staged.at[0, site[2]], w.at[place, pl.ds(0, SENT)], keep_sem).wait()

    def arrive(i, _):
        dc, dz, dy = offset(i)
        source = (core - dc + NC) % NC
        fz, fy = (site[0] - dz + NZ) % NZ, (site[1] - dy + ny) % ny
        at = [labels(source, fz, fy, k) for k in range(NX)]
        spots = [spot(source, *p) for p in at]
        for dx in range(NX):
            if dx == 0:
                @pl.when(i != 0)
                def _():
                    block_copy(i, dx).wait()
            else:
                block_copy(i, dx).wait()
        for k in range(NX):
            unpack(w, spots[k])
        out = fast(start_low, jnp.concatenate([w[p] for p in spots], 1))

        @pl.when(dc == 0)
        def _():
            for k in range(NX):
                acc[(at[k][0] * ny + at[k][1]) * NX + at[k][2]] = out[:, k * LANES : (k + 1) * LANES]

        @pl.when(dc != 0)
        def _():
            for k in range(NX):
                core_out[(at[k][0] - partner_z + NZ) % NZ, at[k][1] * NX + at[k][2]] = out[
                    :, k * LANES : (k + 1) * LANES].astype(BF16)

        return 0

    lax.fori_loop(0, groups // NC, arrive, 0)
    reduce.step()
    lax.fori_loop(groups // NC, groups, arrive, 0)

    lane = lax.broadcasted_iota(jnp.int32, (COLS, LANES), 1)
    spans = n // PER

    def joined_copy(i):
        return pltpu.make_async_copy(
            joined.at[i % 2], blocks_ref.at[:, pl.ds(pl.multiple_of(i * PER * ROWS, LANES), PER * ROWS)],
            join_sem.at[i % 2])

    def join(i, _):
        @pl.when(i >= 2)
        def _():
            joined_copy(i - 2).wait()

        parts = []
        for k in range(PER):
            at = i * PER + k
            r, c = at // (NZ * NYL * NC), at % (NZ * NYL * NC)
            parts.append(spot(c % NC, *labels(c % NC, c // (NYL * NC), (r // NX) * NYL + (c // NC) % NYL, r % NX)))
        for t in range(PER * ROWS // LANES):
            first = w[parts[t]].astype(F32)
            if t:
                first = pltpu.roll(first, LANES - GAP * t, 1)
            after = pltpu.roll(w[parts[t + 1]].astype(F32), ROWS - GAP * t, 1)
            joined[i % 2, :, t * LANES : (t + 1) * LANES] = jnp.where(lane < ROWS - GAP * t, first, after).astype(BF16)
        joined_copy(i).start()
        return 0

    quota = iter([(i * spans // (2 * STEPS), (i + 1) * spans // (2 * STEPS)) for i in range(2 * STEPS)])

    def fill():
        lo, hi = next(quota)
        lax.fori_loop(lo, hi, join, 0)

    z_order = [d % NZ for d in range(1, NZ + 1)]
    for j in range(STEPS):
        done = []
        low = raw[...].astype(BF16)
        if j:
            right[j * B : (j + 1) * B, :] = raw[...]
            gram = dot(raw[...], right[0 : (j + 1) * B, :], NT)
            newest = image_ref[(j - 1) * B : j * B, :]
            reduce = Reduce(jnp.concatenate([gram, dot(newest, image_ref[0 : j * B, :], NT)], 1), j)

        core_copies = {}
        for d in z_order:
            def put(i, value, d=d):
                core_out[d, i] = value.astype(BF16)
            if j:
                product_slab(low, base_of(1 - core, (partner_z + d) % NZ), put)
            core_copies[d] = swap(core_out.at[d], core_in.at[j, d], j, RSC, d)
        if j:
            reduce.step()
        flights = [[] for _ in STREAMS]

        def first(t, d):
            axis = STREAMS[t][2][0]
            flights[t].append(send(out1[t].at[(here[axis] + d) % sizes[axis]], in1[t].at[j, d - 1],
                                   j, RS + t, d, axis))

        for d in z_order:
            core_copies[d].wait_recv()
            at = {"z": (z + d) % NZ}

            def put(i, value, d=d, at=at):
                value = value + core_in[j, d, i].astype(F32)
                at = {"z": at["z"], "y": i // NX, "x": i % NX}
                acc[at["z"] * slab + i] = value
                for t, (lo, hi, (p, q, r)) in enumerate(STREAMS):
                    out1[t][at[p], at[q] * sizes[r] + at[r]] = value[lo:hi].astype(BF16)

            if j:
                product_slab(low, base_of(core, at["z"]), put)
            else:
                for i in range(slab):
                    put(i, acc[at["z"] * slab + i])
            if d:
                first(0, d)
        for t in (1, 2):
            for d in range(1, sizes[STREAMS[t][2][0]]):
                first(t, d)
        done += list(core_copies.values())
        reduce.step()
        fill()
        reduce.step()
        second = [[] for _ in STREAMS]
        for t in (1, 2, 0):
            lo, hi, (p, q, r) = STREAMS[t]
            for copy in flights[t]:
                copy.wait_recv()

            def add(iq, _):
                for ir in range(sizes[r]):
                    at = {p: here[p], q: iq, r: ir}
                    value = acc[(at["z"] * ny + at["y"]) * NX + at["x"], lo:hi]
                    for i in range(sizes[p] - 1):
                        value = value + in1[t][j, i, iq * sizes[r] + ir].astype(F32)
                    out2[t][iq, ir] = value
                return 0

            lax.fori_loop(0, sizes[q], add, 0)
            for d in range(1, sizes[q]):
                second[t].append(send(out2[t].at[(here[q] + d) % sizes[q]], in2[t].at[j, d - 1],
                                      j, RS + 3 + t, d, q))
            done += flights[t]
        reduce.step()
        third = [[] for _ in STREAMS]
        for t in (1, 2, 0):
            lo, hi, (p, q, r) = STREAMS[t]
            for copy in second[t]:
                copy.wait_recv()
            for ir in range(sizes[r]):
                value = out2[t][here[q], ir]
                for i in range(sizes[q] - 1):
                    value = value + in2[t][j, i, ir]
                out3[t][ir] = value
            for d in range(1, sizes[r]):
                third[t].append(send(out3[t].at[(here[r] + d) % sizes[r]], in3[t].at[j, d - 1],
                                     j, RS + 6 + t, d, r))
            done += second[t]
        total = reduce.step()
        done += reduce.sent

        cross = total[:, 0 : j * B]
        clean = total[:, j * B : (j + 1) * B]
        if j:
            gram_ref[(j - 1) * B : j * B, 0 : j * B] = total[:, (j + 1) * B : (2 * j + 1) * B]
            clean = clean - dot(cross, cross, NT)
        solve = inverse_factor(clean)

        parts = []
        for t in range(len(STREAMS)):
            lo, hi, (p, q, r) = STREAMS[t]
            value = out3[t][here[r]]
            for i, copy in enumerate(third[t]):
                copy.wait_recv()
                value = value + in3[t][j, i]
            parts.append(value)
            done += third[t]
        mine = jnp.concatenate(parts, 0)
        if j:
            mine = mine - dot(cross, own[0 : j * B, :])
        mine = dot(solve, mine)
        own[j * B : (j + 1) * B, :] = mine

        gathered[j, core, z, y, x] = mine.astype(BF16)

        def spread(t, phase):
            lo, hi, (p, q, r) = STREAMS[t]
            axis = (r, q, p)[phase]
            free = ("", r, r + q)[phase]
            at = [pl.ds(0, sizes[a]) if a in free else here[a] for a in "zyx"]
            piece = gathered.at[j, core, at[0], at[1], at[2], pl.ds(lo, hi - lo)]
            return [send(piece, piece, j, AG + 3 * phase + t, d, axis) for d in range(1, sizes[axis])]

        flights = [spread(t, 0) for t in range(len(STREAMS))]
        block = raw[...]
        if j:
            block = block - dot(cross, right[0 : j * B, :])
        right[j * B : (j + 1) * B, :] = dot(solve, block)
        for phase in (1, 2):
            for t in (0, 1, 2):
                for copy in flights[t]:
                    copy.wait_recv()
                done += flights[t]
                flights[t] = spread(t, phase)
        fill()
        for t in (1, 2, 0):
            for copy in flights[t]:
                copy.wait_recv()
            done += flights[t]
        handed = []
        for d in range(NZ):
            piece = gathered.at[j, core, (z + d) % NZ]
            handed.append(swap(piece, piece, j, AGC, d))
        done += handed

        def back_slab(total, c, zz):
            wide = [jnp.concatenate([w[base_of(c, zz) + i] for i in range(slab)], 1)]
            for k in range(j + 1):
                wide.append(jnp.concatenate([gathered[k, c, zz, i // NX, i % NX] for i in range(slab)], 1))
            return total + fast(wide[-1], jnp.concatenate(wide, 0), NT)

        total = jnp.zeros((B, COLS + (j + 1) * B), F32)
        total = lax.fori_loop(0, NZ, lambda zz, total: back_slab(total, core, zz), total)

        def handed_in(d, total):
            piece = gathered.at[j, core, (z + d) % NZ]
            pltpu.make_async_remote_copy(
                src_ref=piece, dst_ref=piece, send_sem=send_sem.at[j, AGC, d], recv_sem=recv_sem.at[j, AGC, d],
                device_id=peer("c", 1), device_id_type=MESH).wait_recv()
            return back_slab(total, 1 - core, (partner_z + d) % NZ)

        total = lax.fori_loop(0, NZ, handed_in, total)
        image, grams = total[:, :COLS], total[:, COLS:]

        clean = grams[:, j * B :]
        if j:
            table = coef_ref[0 : j * B, 0 : j * B]
            cross = dot(grams[:, : j * B], table, NT)
            clean = clean - dot(cross, cross, NT)
        solve = inverse_factor(clean)
        if j:
            image = image - dot(cross, image_ref[0 : j * B, :])
        image = dot(solve, image)
        image_ref[j * B : (j + 1) * B, :] = image
        if j + 1 < STEPS:
            raw[...] = image - dot(dot(solve, clean), right[j * B : (j + 1) * B, :])
        left = mine
        if j:
            left = left - dot(cross, left_ref[0 : j * B, :])
            coef_ref[j * B : (j + 1) * B, 0 : j * B] = -dot(solve, dot(cross, table))
        left_ref[j * B : (j + 1) * B, :] = dot(solve, left)
        coef_ref[j * B : (j + 1) * B, j * B : (j + 1) * B] = solve
        for copy in done:
            copy.wait_send()

    reduce = Reduce(dot(image_ref[(STEPS - 1) * B :, :], image_ref[...], NT), STEPS)
    total = None
    while total is None:
        total = reduce.step()
    gram_ref[(STEPS - 1) * B :, :] = total
    for copy in reduce.sent:
        copy.wait_send()
    joined_copy(spans - 2).wait()
    joined_copy(spans - 1).wait()


def chain(start_t, weight):
    ny = NYH * NYL
    slab = ny * NX
    n = NC * NZ * slab
    vmem = pl.BlockSpec(memory_space=pltpu.VMEM)
    hbm = pl.BlockSpec(memory_space=pl.ANY)
    s = STEPS * B
    sizes = {"z": NZ, "y": ny, "x": NX}

    def buffers(shape, kind):
        return [pltpu.VMEM(shape(*(sizes[a] for a in axes)) + (hi - lo, LANES), kind) for lo, hi, axes in STREAMS]

    return pl.pallas_call(
        chain_kernel,
        out_shape=(
            jax.ShapeDtypeStruct((STEPS, NC, NZ, ny, NX, B, LANES), BF16),
            jax.ShapeDtypeStruct((s, LANES), F32),
            jax.ShapeDtypeStruct((s, COLS), F32),
            jax.ShapeDtypeStruct((s, s), F32),
            jax.ShapeDtypeStruct((s, s), F32),
            jax.ShapeDtypeStruct((COLS, n * ROWS), BF16),
        ),
        in_specs=[vmem, hbm],
        out_specs=[vmem] * 5 + [hbm],
        scratch_shapes=[
            pltpu.VMEM((n, COLS, LANES), BF16),
            pltpu.VMEM((2, ROWS, NX * COLS), BF16),
            pltpu.VMEM((n // NX, NX, SENT, LANES), BF16),
            pltpu.VMEM((NZ, slab, B, LANES), BF16),
            pltpu.VMEM((STEPS, NZ, slab, B, LANES), BF16),
            buffers(lambda p, q, r: (p, q * r), BF16),
            buffers(lambda p, q, r: (STEPS, max(p - 1, 1), q * r), BF16),
            buffers(lambda p, q, r: (q, r), F32),
            buffers(lambda p, q, r: (STEPS, max(q - 1, 1), r), F32),
            buffers(lambda p, q, r: (r,), F32),
            buffers(lambda p, q, r: (STEPS, max(r - 1, 1)), F32),
            pltpu.VMEM((NZ * slab, B, LANES), F32),
            pltpu.VMEM((STEPS + 1, 4, B, 3 * LANES), F32),
            pltpu.VMEM((STEPS + 1, 5, 3, B, 3 * LANES), F32),
            pltpu.VMEM((s, COLS), F32),
            pltpu.VMEM((B, COLS), F32),
            pltpu.VMEM((s, LANES), F32),
            pltpu.VMEM((2, COLS, PER * ROWS), BF16),
            pltpu.SemaphoreType.DMA((2,)),
            pltpu.SemaphoreType.DMA((2,)),
            pltpu.SemaphoreType.DMA,
            pltpu.SemaphoreType.DMA((n // NX, NX)),
            pltpu.SemaphoreType.DMA((n // NX, NX)),
            pltpu.SemaphoreType.DMA((STEPS + 1, EXCHANGES, 4)),
            pltpu.SemaphoreType.DMA((STEPS + 1, EXCHANGES, 4)),
        ],
        compiler_params=pltpu.CompilerParams(
            collective_id=0, has_side_effects=True, vmem_limit_bytes=62 * 1024 * 1024),
    )(start_t, weight)


def sweeps(gram_ref, coef_ref):
    g = [[None] * STEPS for _ in range(STEPS)]
    for i in range(STEPS):
        for k in range(i + 1):
            g[i][k] = gram_ref[i * B : (i + 1) * B, k * B : (k + 1) * B]
            if k < i:
                g[k][i] = g[i][k].T
    whole = jnp.concatenate([jnp.concatenate(r, 1) for r in g], 0)

    def orth(grown):
        top, bottom = grown[:B], grown[B:]
        one = inverse_factor(dot(top, top, NT))
        first = dot(one, top)
        cross = dot(bottom, first, NT)
        clean = bottom - dot(cross, first)
        two = inverse_factor(dot(clean, clean, NT))
        return jnp.concatenate([first, dot(two, clean)], 0)

    basis = orth(whole[:RANK])
    return lax.fori_loop(1, SWEEPS, lambda _, basis: orth(dot(basis, whole)), basis)


def finish_kernel(gram_in, coef_in, left_in, image_in, gathered_in, weight, adapter_left, adapter_right, out,
                  gram_ref, coef_ref, left_ref, image_ref, gathered, strips, high, low, right,
                  small_sem, big_sem, load_sem, out_sem):
    width = PER * ROWS
    smalls = [pltpu.make_async_copy(src, dst, small_sem.at[i]) for i, (src, dst) in enumerate(
        ((gram_in, gram_ref), (coef_in, coef_ref), (left_in, left_ref), (image_in, image_ref)))]
    for copy in smalls:
        copy.start()
    big = pltpu.make_async_copy(gathered_in, gathered, big_sem)
    big.start()

    def place(ref, i):
        return ref.at[:, pl.ds(pl.multiple_of(i * width, LANES), width)]

    def load(i):
        return pltpu.make_async_copy(place(weight, i), strips.at[i], load_sem.at[i])

    def store(i):
        return pltpu.make_async_copy(strips.at[i], place(out, i), out_sem.at[i])

    def each(body):
        lax.fori_loop(0, strips.shape[0], lambda i, _: (body(i), 0)[1], 0)

    each(lambda i: load(i).start())
    for copy in smalls:
        copy.wait()
    basis = sweeps(gram_ref, coef_ref)
    adapter_left[...] = dot(basis, left_ref[...]).T[:ROWS]
    wide = dot(basis, image_ref[...]).T
    adapter_right[...] = wide
    right[...] = wide.astype(BF16)
    mixed = dot(basis, coef_ref[...])
    high[...] = mixed.astype(BF16)
    low[...] = (mixed - mixed.astype(BF16).astype(F32)).astype(BF16)
    big.wait()

    def residual(i):
        pieces = []
        for k in range(PER):
            at = i * PER + k
            r, c = at // (NZ * NYL * NC), at % (NZ * NYL * NC)
            core = c % NC
            where = labels(core, c // (NYL * NC), (r // NX) * NYL + (c // NC) % NYL, r % NX)
            pieces.append(jnp.concatenate([gathered[(s, core) + where] for s in range(STEPS)], 0))
        stacked = jnp.concatenate(pieces, 1)
        left = (fast(high[...], stacked) + fast(low[...], stacked)).astype(BF16).T
        left = jnp.concatenate([left[k * LANES : k * LANES + ROWS] for k in range(PER)], 0)
        load(i).wait()
        strips[i] = (strips[i].astype(F32) - fast(right[...], left, NT)).astype(BF16)
        store(i).start()

    each(residual)
    each(lambda i: store(i).wait())


def finish(gram, coef, left, images, gathered, blocks):
    rows = blocks.shape[1]
    n = rows // (PER * ROWS)
    s = STEPS * B
    vmem = pl.BlockSpec(memory_space=pltpu.VMEM)
    hbm = pl.BlockSpec(memory_space=pl.ANY)
    held = [pltpu.VMEM(a.shape, a.dtype) for a in (gram, coef, left, images, gathered)]
    return pl.pallas_call(
        finish_kernel,
        out_shape=(
            jax.ShapeDtypeStruct((ROWS, RANK), F32),
            jax.ShapeDtypeStruct((COLS, RANK), F32),
            jax.ShapeDtypeStruct((COLS, rows), BF16),
        ),
        in_specs=[hbm] * 6,
        out_specs=(vmem, vmem, hbm),
        scratch_shapes=held + [
            pltpu.VMEM((n, COLS, PER * ROWS), BF16),
            pltpu.VMEM((RANK, s), BF16), pltpu.VMEM((RANK, s), BF16), pltpu.VMEM((COLS, RANK), BF16),
            pltpu.SemaphoreType.DMA((4,)), pltpu.SemaphoreType.DMA, pltpu.SemaphoreType.DMA((n,)),
            pltpu.SemaphoreType.DMA((n,)),
        ],
        compiler_params=pltpu.CompilerParams(vmem_limit_bytes=60 * 1024 * 1024),
    )(gram, coef, left, images, gathered, blocks)


def shards(weight, start):
    gathered, left, images, gram, coef, blocks = chain(start.T, weight)
    adapter_left, adapter_right, out = finish(gram, coef, left, images, gathered, blocks)
    return (adapter_left, adapter_right, out.T)


def solution(mesh):
    return jax.shard_map(
        shards,
        mesh=mesh,
        in_specs=(P(("row", "col"), None), P(("col", "row"), None)),
        out_specs=(P(("row", "col"), None), P(("col", "row"), None), P(None, ("col", "row"))),
        check_vma=False,
    )
```

```python
import functools

import jax
import jax.numpy as jnp
from jax import lax
from jax.experimental import pallas as pl
from jax.experimental.pallas import tpu as pltpu
from jax.sharding import PartitionSpec as P

STEPS = 3
RANK = 128
PER = 8
SWEEPS = 4
B = 64
LANES = 128

NX, NYH, NYL, NZ, NC = 4, 2, 2, 4, 2
ROWS, COLS = 112, 416
GAP, TAIL = LANES - ROWS, 48
SENT = COLS - TAIL

HIGHEST = lax.Precision.HIGHEST
MESH = pl.DeviceIdType.MESH
F32 = jnp.float32
BF16 = jnp.bfloat16
NT = (((1,), (1,)), ((), ()))
NN = (((1,), (0,)), ((), ()))

STREAMS = ((0, 32, "zyx"), (32, 48, "yxz"), (48, 64, "xzy"))
RSC, RS, AG, AGC, ARC, ARZ, ARY, ARX, ARB = 0, 1, 10, 19, 20, 21, 22, 23, 24
EXCHANGES = 25


def dot(left, right, dims=NN):
    return lax.dot_general(left, right, dims, precision=HIGHEST, preferred_element_type=F32)


def fast(left, right, dims=NN):
    return lax.dot_general(left, right, dims, preferred_element_type=F32)


def inverse_factor(gram):
    sub = lax.broadcasted_iota(jnp.int32, (8, LANES), 0)
    lane = lax.broadcasted_iota(jnp.int32, (8, LANES), 1)
    wide = jnp.concatenate([gram, jnp.zeros_like(gram)], 1)
    n = B // 8
    rows = [jnp.where(lane == sub + (B + 8 * q), 1.0, wide[8 * q : 8 * q + 8]) for q in range(n)]
    for p in range(n):
        columns = {q: [jnp.broadcast_to(rows[q][:, 8 * p + k : 8 * p + k + 1], (8, LANES)) for k in range(8)]
                   for q in range(p, n)}
        scale = jnp.ones((8, LANES), F32)
        for k in range(8):
            pivot = columns[p][k][k : k + 1]
            inverse = 1.0 / pivot
            scale = jnp.where(sub == k, lax.rsqrt(pivot), scale)
            row = rows[p][k : k + 1] * inverse
            ahead = {i: columns[p][i][k : k + 1] * inverse for i in range(k + 1, 8)}
            for q in range(p, n):
                factor = columns[q][k]
                if q == p:
                    factor = jnp.where(sub > k, factor, 0.0)
                rows[q] = rows[q] - factor * row
                for i in range(k + 1, 8):
                    columns[q][i] = columns[q][i] - factor * ahead[i]
        rows[p] = rows[p] * scale
    return jnp.concatenate(rows, 0)[:, B:]


def pack(block):
    tail = block[SENT:].astype(F32)
    lane = lax.broadcasted_iota(jnp.int32, (TAIL, LANES), 1)
    pieces = []
    for m in range(ROWS // GAP):
        moved = pltpu.roll(tail, ROWS - GAP * m, 1)
        pieces.append(jnp.where(lane < ROWS, block[TAIL * m : TAIL * (m + 1)].astype(F32), moved).astype(BF16))
    return jnp.concatenate(pieces + [block[TAIL * (ROWS // GAP) : SENT]], 0)


def unpack(w, p):
    lane = lax.broadcasted_iota(jnp.int32, (TAIL, LANES), 1)
    tail = jnp.zeros((TAIL, LANES), F32)
    for m in range(ROWS // GAP):
        at = slice(TAIL * m, TAIL * (m + 1))
        piece = w[p, at].astype(F32)
        moved = pltpu.roll(piece, (LANES - ROWS + GAP * m) % LANES, 1)
        tail = jnp.where((lane >= GAP * m) & (lane < GAP * (m + 1)), moved, tail)
        w[p, at] = jnp.where(lane < ROWS, piece, 0.0).astype(BF16)
    w[p, SENT:] = tail.astype(BF16)


def chain_kernel(start_ref, weight_ref, gathered, left_ref, image_ref, gram_ref, coef_ref, blocks_ref,
                 w, strip, staged, core_out, core_in, out1, in1, out2, in2, out3, in3, acc,
                 ar_out, ar_in, right, raw, own, joined, join_sem, strip_sem, keep_sem, put_sem, get_sem, send_sem, recv_sem):
    ny = NYH * NYL
    slab = ny * NX
    n = NC * NZ * slab
    row_id = lax.axis_index("row")
    col_id = lax.axis_index("col")
    y_hi, x = row_id // NX, row_id % NX
    z, y_lo, core = col_id // (NYL * NC), (col_id // NC) % NYL, col_id % NC
    y = y_hi * NYL + y_lo
    here = {"z": z, "y": y, "x": x}
    sizes = {"c": NC, "z": NZ, "y": ny, "x": NX}

    def device(core, z, y, x):
        return ((y // NYL) * NX + x, (z * NYL + y % NYL) * NC + core)

    def spot(core, z, y, x):
        return ((core * NZ + z) * ny + y) * NX + x

    def peer(axis, d):
        if axis == "c":
            return device((core + d) % NC, z, y, x)
        if axis == "z":
            return device(core, (z + d) % NZ, y, x)
        if axis == "y":
            return device(core, z, (y + d) % ny, x)
        return device(core, z, y, (x + d) % NX)

    place = spot(core, z, y, x)

    groups = n // NX

    def offset(i):
        step, g = i // ny, i % ny
        return step // NZ, (g + step % NZ) % NZ, g

    def strip_copy(i):
        dc, dz, dy = offset(i)
        dr, dl = device((core + dc) % NC, (z + dz) % NZ, (y + dy) % ny, 0)
        block = dl * (NYH * NX) + dr
        return pltpu.make_async_copy(
            weight_ref.at[:, pl.ds(pl.multiple_of(block * COLS, LANES), NX * COLS)], strip.at[i % 2],
            strip_sem.at[i % 2])

    def block_copy(i, dx):
        dc, dz, dy = offset(i)
        tx = (x + dx) % NX
        return pltpu.make_async_remote_copy(
            src_ref=staged.at[i, tx], dst_ref=w.at[place, pl.ds(0, SENT)], send_sem=put_sem.at[i, dx], recv_sem=get_sem.at[i, dx],
            device_id=device((core + dc) % NC, (z + dz) % NZ, (y + dy) % ny, tx), device_id_type=MESH)

    strip_copy(0).start()
    barrier = pltpu.get_barrier_semaphore()

    def greet(d, _):
        to = (place + d) % n
        target = device(to // (NZ * slab), (to // slab) % NZ, (to // NX) % ny, to % NX)
        pl.semaphore_signal(barrier, inc=1, device_id=target, device_id_type=MESH)
        return 0

    lax.fori_loop(1, n, greet, 0)

    def stage(i):
        strip_copy(i).wait()

        @pl.when(i < groups - 1)
        def _():
            strip_copy(i + 1).start()

        value = strip[i % 2]
        value = jnp.concatenate([value, jnp.zeros((LANES - ROWS, NX * COLS), BF16)], 0).T
        for k in range(NX):
            staged[i, k] = pack(value[k * COLS : (k + 1) * COLS])

    def scatter(step, _):
        def each(g, _):
            stage(step * ny + g)
            return 0

        lax.fori_loop(0, ny, each, 0)

        @pl.when(step == 0)
        def _():
            pl.semaphore_wait(barrier, n - 1)
            pltpu.make_async_copy(staged.at[0, x], w.at[place, pl.ds(0, SENT)], keep_sem).start()

        def rotate(a, _):
            for dx in range(NX):
                i = step * ny + (dx + a) % ny
                if dx == 0:
                    @pl.when(i != 0)
                    def _():
                        block_copy(i, dx).start()
                else:
                    block_copy(i, dx).start()
            return 0

        lax.fori_loop(0, ny, rotate, 0)
        return 0

    lax.fori_loop(0, groups // ny, scatter, 0)

    def send_to(target, src, dst, j, phase, d):
        copy = pltpu.make_async_remote_copy(
            src_ref=src, dst_ref=dst, send_sem=send_sem.at[j, phase, d], recv_sem=recv_sem.at[j, phase, d],
            device_id=target, device_id_type=MESH)
        copy.start()
        return copy

    def send(src, dst, j, phase, d, axis):
        return send_to(peer(axis, d), src, dst, j, phase, d)

    def swap(src, dst, j, phase, d):
        return send_to(peer("c", 1), src, dst, j, phase, d)

    half = B // NC
    others = {"z": ARZ, "y": ARY, "x": ARX}

    class Reduce:
        def __init__(self, value, j):
            self.j, self.lanes, self.stage = j, value.shape[1], 0
            self.sent = []
            pad = -self.lanes % LANES
            if pad:
                value = jnp.concatenate([value, jnp.zeros((B, pad), F32)], 1)
            self.width = value.shape[1]
            out = ar_out.at[j, 0]
            out[:, : self.width] = value
            mine = pl.ds(pl.multiple_of(core * half, half), half)
            theirs = pl.ds(pl.multiple_of((1 - core) * half, half), half)
            self.mine = mine
            self.pending = [send(ar_out.at[j, 0, theirs, pl.ds(0, self.width)],
                                 ar_in.at[j, 0, 0, pl.ds(0, half), pl.ds(0, self.width)], j, ARC, 1, "c")]
            self.own = out[mine, : self.width]

        def step(self):
            j, width, s = self.j, self.width, self.stage
            total = self.own
            for i, copy in enumerate(self.pending):
                copy.wait_recv()
                if s < 4:
                    total = total + ar_in[j, s, i, 0:half, 0:width]
            self.sent += self.pending
            self.pending = []
            self.stage += 1
            if s < 3:
                axis = "zyx"[s]
                self.own = total
                ar_out[j, s + 1, 0:half, 0:width] = total
                for d in range(1, sizes[axis]):
                    self.pending.append(send(
                        ar_out.at[j, s + 1, pl.ds(0, half), pl.ds(0, width)],
                        ar_in.at[j, s + 1, d - 1, pl.ds(0, half), pl.ds(0, width)], j, others[axis], d, axis))
            elif s == 3:
                ar_in[j, 4, 0, self.mine, 0:width] = total
                there = ar_in.at[j, 4, 0, self.mine, pl.ds(0, width)]
                self.pending.append(send(there, there, j, ARB, 1, "c"))
            else:
                return ar_in[j, 4, 0, :, 0 : self.lanes]
            return None

    def product_slab(low, base, put):
        out = fast(low, jnp.concatenate([w[base + i] for i in range(slab)], 1))
        for i in range(slab):
            put(i, out[:, i * LANES : (i + 1) * LANES])

    def base_of(c, zz):
        return (c * NZ + zz) * slab

    raw[...] = start_ref[...]
    coef_ref[...] = jnp.zeros_like(coef_ref)
    start_low = raw[...].astype(BF16)
    right[0:B, :] = raw[...]
    reduce = Reduce(dot(raw[...], raw[...], NT), 0)
    pltpu.make_async_copy(staged.at[0, x], w.at[place, pl.ds(0, SENT)], keep_sem).wait()

    def arrive(i, _):
        dc, dz, dy = offset(i)
        fz, fy = (z - dz + NZ) % NZ, (y - dy + ny) % ny
        base = spot((core - dc + NC) % NC, fz, fy, 0)
        for dx in range(NX):
            if dx == 0:
                @pl.when(i != 0)
                def _():
                    block_copy(i, dx).wait()
            else:
                block_copy(i, dx).wait()
        for k in range(NX):
            unpack(w, base + k)
        out = fast(start_low, jnp.concatenate([w[base + k] for k in range(NX)], 1))

        @pl.when(dc == 0)
        def _():
            for k in range(NX):
                acc[(fz * ny + fy) * NX + k] = out[:, k * LANES : (k + 1) * LANES]

        @pl.when(dc != 0)
        def _():
            for k in range(NX):
                core_out[(NZ - dz) % NZ, fy * NX + k] = out[:, k * LANES : (k + 1) * LANES].astype(BF16)

        return 0

    lax.fori_loop(0, groups // NC, arrive, 0)
    reduce.step()
    lax.fori_loop(groups // NC, groups, arrive, 0)

    lane = lax.broadcasted_iota(jnp.int32, (COLS, LANES), 1)
    spans = n // PER

    def joined_copy(i):
        return pltpu.make_async_copy(
            joined.at[i % 2], blocks_ref.at[:, pl.ds(pl.multiple_of(i * PER * ROWS, LANES), PER * ROWS)],
            join_sem.at[i % 2])

    def join(i, _):
        @pl.when(i >= 2)
        def _():
            joined_copy(i - 2).wait()

        parts = []
        for k in range(PER):
            at = i * PER + k
            r, c = at // (NZ * NYL * NC), at % (NZ * NYL * NC)
            parts.append(spot(c % NC, c // (NYL * NC), (r // NX) * NYL + (c // NC) % NYL, r % NX))
        for t in range(PER * ROWS // LANES):
            first = w[parts[t]].astype(F32)
            if t:
                first = pltpu.roll(first, LANES - GAP * t, 1)
            after = pltpu.roll(w[parts[t + 1]].astype(F32), ROWS - GAP * t, 1)
            joined[i % 2, :, t * LANES : (t + 1) * LANES] = jnp.where(lane < ROWS - GAP * t, first, after).astype(BF16)
        joined_copy(i).start()
        return 0

    quota = iter([(i * spans // (2 * STEPS), (i + 1) * spans // (2 * STEPS)) for i in range(2 * STEPS)])

    def fill():
        lo, hi = next(quota)
        lax.fori_loop(lo, hi, join, 0)

    z_order = [d % NZ for d in range(1, NZ + 1)]
    for j in range(STEPS):
        done = []
        low = raw[...].astype(BF16)
        if j:
            right[j * B : (j + 1) * B, :] = raw[...]
            gram = dot(raw[...], right[0 : (j + 1) * B, :], NT)
            newest = image_ref[(j - 1) * B : j * B, :]
            reduce = Reduce(jnp.concatenate([gram, dot(newest, image_ref[0 : j * B, :], NT)], 1), j)

        core_copies = {}
        for d in z_order:
            def put(i, value, d=d):
                core_out[d, i] = value.astype(BF16)
            if j:
                product_slab(low, base_of(1 - core, (z + d) % NZ), put)
            core_copies[d] = swap(core_out.at[d], core_in.at[j, d], j, RSC, d)
        if j:
            reduce.step()
        flights = [[] for _ in STREAMS]

        def first(t, d):
            axis = STREAMS[t][2][0]
            flights[t].append(send(out1[t].at[(here[axis] + d) % sizes[axis]], in1[t].at[j, d - 1],
                                   j, RS + t, d, axis))

        for d in z_order:
            core_copies[d].wait_recv()
            at = {"z": (z + d) % NZ}

            def put(i, value, d=d, at=at):
                value = value + core_in[j, d, i].astype(F32)
                at = {"z": at["z"], "y": i // NX, "x": i % NX}
                acc[at["z"] * slab + i] = value
                for t, (lo, hi, (p, q, r)) in enumerate(STREAMS):
                    out1[t][at[p], at[q] * sizes[r] + at[r]] = value[lo:hi].astype(BF16)

            if j:
                product_slab(low, base_of(core, at["z"]), put)
            else:
                for i in range(slab):
                    put(i, acc[at["z"] * slab + i])
            if d:
                first(0, d)
        for t in (1, 2):
            for d in range(1, sizes[STREAMS[t][2][0]]):
                first(t, d)
        done += list(core_copies.values())
        reduce.step()
        fill()
        reduce.step()
        second = [[] for _ in STREAMS]
        for t in (1, 2, 0):
            lo, hi, (p, q, r) = STREAMS[t]
            for copy in flights[t]:
                copy.wait_recv()

            def add(iq, _):
                for ir in range(sizes[r]):
                    at = {p: here[p], q: iq, r: ir}
                    value = acc[(at["z"] * ny + at["y"]) * NX + at["x"], lo:hi]
                    for i in range(sizes[p] - 1):
                        value = value + in1[t][j, i, iq * sizes[r] + ir].astype(F32)
                    out2[t][iq, ir] = value
                return 0

            lax.fori_loop(0, sizes[q], add, 0)
            for d in range(1, sizes[q]):
                second[t].append(send(out2[t].at[(here[q] + d) % sizes[q]], in2[t].at[j, d - 1],
                                      j, RS + 3 + t, d, q))
            done += flights[t]
        reduce.step()
        third = [[] for _ in STREAMS]
        for t in (1, 2, 0):
            lo, hi, (p, q, r) = STREAMS[t]
            for copy in second[t]:
                copy.wait_recv()
            for ir in range(sizes[r]):
                value = out2[t][here[q], ir]
                for i in range(sizes[q] - 1):
                    value = value + in2[t][j, i, ir]
                out3[t][ir] = value
            for d in range(1, sizes[r]):
                third[t].append(send(out3[t].at[(here[r] + d) % sizes[r]], in3[t].at[j, d - 1],
                                     j, RS + 6 + t, d, r))
            done += second[t]
        total = reduce.step()
        done += reduce.sent

        cross = total[:, 0 : j * B]
        clean = total[:, j * B : (j + 1) * B]
        if j:
            gram_ref[(j - 1) * B : j * B, 0 : j * B] = total[:, (j + 1) * B : (2 * j + 1) * B]
            clean = clean - dot(cross, cross, NT)
        solve = inverse_factor(clean)

        parts = []
        for t in range(len(STREAMS)):
            lo, hi, (p, q, r) = STREAMS[t]
            value = out3[t][here[r]]
            for i, copy in enumerate(third[t]):
                copy.wait_recv()
                value = value + in3[t][j, i]
            parts.append(value)
            done += third[t]
        mine = jnp.concatenate(parts, 0)
        if j:
            mine = mine - dot(cross, own[0 : j * B, :])
        mine = dot(solve, mine)
        own[j * B : (j + 1) * B, :] = mine

        gathered[j, core, z, y, x] = mine.astype(BF16)

        def spread(t, phase):
            lo, hi, (p, q, r) = STREAMS[t]
            axis = (r, q, p)[phase]
            free = ("", r, r + q)[phase]
            at = [pl.ds(0, sizes[a]) if a in free else here[a] for a in "zyx"]
            piece = gathered.at[j, core, at[0], at[1], at[2], pl.ds(lo, hi - lo)]
            return [send(piece, piece, j, AG + 3 * phase + t, d, axis) for d in range(1, sizes[axis])]

        flights = [spread(t, 0) for t in range(len(STREAMS))]
        block = raw[...]
        if j:
            block = block - dot(cross, right[0 : j * B, :])
        right[j * B : (j + 1) * B, :] = dot(solve, block)
        for phase in (1, 2):
            for t in (0, 1, 2):
                for copy in flights[t]:
                    copy.wait_recv()
                done += flights[t]
                flights[t] = spread(t, phase)
        fill()
        for t in (1, 2, 0):
            for copy in flights[t]:
                copy.wait_recv()
            done += flights[t]
        handed = []
        for d in range(NZ):
            piece = gathered.at[j, core, (z + d) % NZ]
            handed.append(swap(piece, piece, j, AGC, d))
        done += handed

        def back_slab(total, c, zz):
            wide = [jnp.concatenate([w[base_of(c, zz) + i] for i in range(slab)], 1)]
            for k in range(j + 1):
                wide.append(jnp.concatenate([gathered[k, c, zz, i // NX, i % NX] for i in range(slab)], 1))
            return total + fast(wide[-1], jnp.concatenate(wide, 0), NT)

        total = jnp.zeros((B, COLS + (j + 1) * B), F32)
        total = lax.fori_loop(0, NZ, lambda zz, total: back_slab(total, core, zz), total)

        def handed_in(d, total):
            piece = gathered.at[j, core, (z + d) % NZ]
            pltpu.make_async_remote_copy(
                src_ref=piece, dst_ref=piece, send_sem=send_sem.at[j, AGC, d], recv_sem=recv_sem.at[j, AGC, d],
                device_id=peer("c", 1), device_id_type=MESH).wait_recv()
            return back_slab(total, 1 - core, (z + d) % NZ)

        total = lax.fori_loop(0, NZ, handed_in, total)
        image, grams = total[:, :COLS], total[:, COLS:]

        clean = grams[:, j * B :]
        if j:
            table = coef_ref[0 : j * B, 0 : j * B]
            cross = dot(grams[:, : j * B], table, NT)
            clean = clean - dot(cross, cross, NT)
        solve = inverse_factor(clean)
        if j:
            image = image - dot(cross, image_ref[0 : j * B, :])
        image = dot(solve, image)
        image_ref[j * B : (j + 1) * B, :] = image
        if j + 1 < STEPS:
            raw[...] = image - dot(dot(solve, clean), right[j * B : (j + 1) * B, :])
        left = mine
        if j:
            left = left - dot(cross, left_ref[0 : j * B, :])
            coef_ref[j * B : (j + 1) * B, 0 : j * B] = -dot(solve, dot(cross, table))
        left_ref[j * B : (j + 1) * B, :] = dot(solve, left)
        coef_ref[j * B : (j + 1) * B, j * B : (j + 1) * B] = solve
        for copy in done:
            copy.wait_send()

    reduce = Reduce(dot(image_ref[(STEPS - 1) * B :, :], image_ref[...], NT), STEPS)
    total = None
    while total is None:
        total = reduce.step()
    gram_ref[(STEPS - 1) * B :, :] = total
    for copy in reduce.sent:
        copy.wait_send()
    joined_copy(spans - 2).wait()
    joined_copy(spans - 1).wait()


def chain(start_t, weight):
    ny = NYH * NYL
    slab = ny * NX
    n = NC * NZ * slab
    vmem = pl.BlockSpec(memory_space=pltpu.VMEM)
    hbm = pl.BlockSpec(memory_space=pl.ANY)
    s = STEPS * B
    sizes = {"z": NZ, "y": ny, "x": NX}

    def buffers(shape, kind):
        return [pltpu.VMEM(shape(*(sizes[a] for a in axes)) + (hi - lo, LANES), kind) for lo, hi, axes in STREAMS]

    return pl.pallas_call(
        chain_kernel,
        out_shape=(
            jax.ShapeDtypeStruct((STEPS, NC, NZ, ny, NX, B, LANES), BF16),
            jax.ShapeDtypeStruct((s, LANES), F32),
            jax.ShapeDtypeStruct((s, COLS), F32),
            jax.ShapeDtypeStruct((s, s), F32),
            jax.ShapeDtypeStruct((s, s), F32),
            jax.ShapeDtypeStruct((COLS, n * ROWS), BF16),
        ),
        in_specs=[vmem, hbm],
        out_specs=[vmem] * 5 + [hbm],
        scratch_shapes=[
            pltpu.VMEM((n, COLS, LANES), BF16),
            pltpu.VMEM((2, ROWS, NX * COLS), BF16),
            pltpu.VMEM((n // NX, NX, SENT, LANES), BF16),
            pltpu.VMEM((NZ, slab, B, LANES), BF16),
            pltpu.VMEM((STEPS, NZ, slab, B, LANES), BF16),
            buffers(lambda p, q, r: (p, q * r), BF16),
            buffers(lambda p, q, r: (STEPS, max(p - 1, 1), q * r), BF16),
            buffers(lambda p, q, r: (q, r), F32),
            buffers(lambda p, q, r: (STEPS, max(q - 1, 1), r), F32),
            buffers(lambda p, q, r: (r,), F32),
            buffers(lambda p, q, r: (STEPS, max(r - 1, 1)), F32),
            pltpu.VMEM((NZ * slab, B, LANES), F32),
            pltpu.VMEM((STEPS + 1, 4, B, 3 * LANES), F32),
            pltpu.VMEM((STEPS + 1, 5, 3, B, 3 * LANES), F32),
            pltpu.VMEM((s, COLS), F32),
            pltpu.VMEM((B, COLS), F32),
            pltpu.VMEM((s, LANES), F32),
            pltpu.VMEM((2, COLS, PER * ROWS), BF16),
            pltpu.SemaphoreType.DMA((2,)),
            pltpu.SemaphoreType.DMA((2,)),
            pltpu.SemaphoreType.DMA,
            pltpu.SemaphoreType.DMA((n // NX, NX)),
            pltpu.SemaphoreType.DMA((n // NX, NX)),
            pltpu.SemaphoreType.DMA((STEPS + 1, EXCHANGES, 4)),
            pltpu.SemaphoreType.DMA((STEPS + 1, EXCHANGES, 4)),
        ],
        compiler_params=pltpu.CompilerParams(
            collective_id=0, has_side_effects=True, vmem_limit_bytes=62 * 1024 * 1024),
    )(start_t, weight)


def sweeps(gram_ref, coef_ref):
    g = [[None] * STEPS for _ in range(STEPS)]
    for i in range(STEPS):
        for k in range(i + 1):
            g[i][k] = gram_ref[i * B : (i + 1) * B, k * B : (k + 1) * B]
            if k < i:
                g[k][i] = g[i][k].T
    whole = jnp.concatenate([jnp.concatenate(r, 1) for r in g], 0)

    def orth(grown):
        top, bottom = grown[:B], grown[B:]
        one = inverse_factor(dot(top, top, NT))
        first = dot(one, top)
        cross = dot(bottom, first, NT)
        clean = bottom - dot(cross, first)
        two = inverse_factor(dot(clean, clean, NT))
        return jnp.concatenate([first, dot(two, clean)], 0)

    basis = orth(whole[:RANK])
    return lax.fori_loop(1, SWEEPS, lambda _, basis: orth(dot(basis, whole)), basis)


def finish_kernel(gram_in, coef_in, left_in, image_in, gathered_in, weight, adapter_left, adapter_right, out,
                  gram_ref, coef_ref, left_ref, image_ref, gathered, strips, high, low, right,
                  small_sem, big_sem, load_sem, out_sem):
    width = PER * ROWS
    smalls = [pltpu.make_async_copy(src, dst, small_sem.at[i]) for i, (src, dst) in enumerate(
        ((gram_in, gram_ref), (coef_in, coef_ref), (left_in, left_ref), (image_in, image_ref)))]
    for copy in smalls:
        copy.start()
    big = pltpu.make_async_copy(gathered_in, gathered, big_sem)
    big.start()

    def place(ref, i):
        return ref.at[:, pl.ds(pl.multiple_of(i * width, LANES), width)]

    def load(i):
        return pltpu.make_async_copy(place(weight, i), strips.at[i], load_sem.at[i])

    def store(i):
        return pltpu.make_async_copy(strips.at[i], place(out, i), out_sem.at[i])

    def each(body):
        lax.fori_loop(0, strips.shape[0], lambda i, _: (body(i), 0)[1], 0)

    each(lambda i: load(i).start())
    for copy in smalls:
        copy.wait()
    basis = sweeps(gram_ref, coef_ref)
    adapter_left[...] = dot(basis, left_ref[...]).T[:ROWS]
    wide = dot(basis, image_ref[...]).T
    adapter_right[...] = wide
    right[...] = wide.astype(BF16)
    mixed = dot(basis, coef_ref[...])
    high[...] = mixed.astype(BF16)
    low[...] = (mixed - mixed.astype(BF16).astype(F32)).astype(BF16)
    big.wait()

    def residual(i):
        pieces = []
        for k in range(PER):
            at = i * PER + k
            r, c = at // (NZ * NYL * NC), at % (NZ * NYL * NC)
            core = c % NC
            where = (c // (NYL * NC), (r // NX) * NYL + (c // NC) % NYL, r % NX)
            pieces.append(jnp.concatenate([gathered[(s, core) + where] for s in range(STEPS)], 0))
        stacked = jnp.concatenate(pieces, 1)
        left = (fast(high[...], stacked) + fast(low[...], stacked)).astype(BF16).T
        left = jnp.concatenate([left[k * LANES : k * LANES + ROWS] for k in range(PER)], 0)
        load(i).wait()
        strips[i] = (strips[i].astype(F32) - fast(right[...], left, NT)).astype(BF16)
        store(i).start()

    each(residual)
    each(lambda i: store(i).wait())


def finish(gram, coef, left, images, gathered, blocks):
    rows = blocks.shape[1]
    n = rows // (PER * ROWS)
    s = STEPS * B
    vmem = pl.BlockSpec(memory_space=pltpu.VMEM)
    hbm = pl.BlockSpec(memory_space=pl.ANY)
    held = [pltpu.VMEM(a.shape, a.dtype) for a in (gram, coef, left, images, gathered)]
    return pl.pallas_call(
        finish_kernel,
        out_shape=(
            jax.ShapeDtypeStruct((ROWS, RANK), F32),
            jax.ShapeDtypeStruct((COLS, RANK), F32),
            jax.ShapeDtypeStruct((COLS, rows), BF16),
        ),
        in_specs=[hbm] * 6,
        out_specs=(vmem, vmem, hbm),
        scratch_shapes=held + [
            pltpu.VMEM((n, COLS, PER * ROWS), BF16),
            pltpu.VMEM((RANK, s), BF16), pltpu.VMEM((RANK, s), BF16), pltpu.VMEM((COLS, RANK), BF16),
            pltpu.SemaphoreType.DMA((4,)), pltpu.SemaphoreType.DMA, pltpu.SemaphoreType.DMA((n,)),
            pltpu.SemaphoreType.DMA((n,)),
        ],
        compiler_params=pltpu.CompilerParams(vmem_limit_bytes=60 * 1024 * 1024),
    )(gram, coef, left, images, gathered, blocks)


def shards(weight, start):
    gathered, left, images, gram, coef, blocks = chain(start.T, weight)
    adapter_left, adapter_right, out = finish(gram, coef, left, images, gathered, blocks)
    return (adapter_left, adapter_right, out.T)


def solution(mesh):
    return jax.shard_map(
        shards,
        mesh=mesh,
        in_specs=(P(("row", "col"), None), P(("col", "row"), None)),
        out_specs=(P(("row", "col"), None), P(("col", "row"), None), P(None, ("col", "row"))),
        check_vma=False,
    )
```
